512 devices in a mesh: row: 32 (over y, x, core), col: 16 (over z).
Axes of the slice: x: 4, y: 4, z: 16, core: 2. Of those that a mesh axis runs over, the one named last changes fastest.
Arguments:
- tokens: bfloat16 [4096, 6144], P('row', 'col'), may hold values from -6 to 6
- weight_blocks: bfloat16 [16, 128, 4096], P('col', 'row'), may hold values from -0.375 to 0.375
- block_rows: int32 [16, 128], P('col', 'row'), may hold values from 0 to 95, as said below
- block_columns: int32 [16, 128], P('col', 'row'), may hold values from 0 to 47
- panel_counts: int32 [16], P('col'), may hold values from 16 to 128, as said below
- hidden_grad: bfloat16 [4096, 49152], P('row', 'col'), may hold values from -1.1953125 to 1.1953125
Outputs:
- hidden: bfloat16 [4096, 49152], P('row', 'col')
- input_grad: bfloat16 [4096, 6144], P('row', 'col')
- weight_grad: bfloat16 [16, 128, 4096], P('col', 'row')
The draws below stay inside these ranges and needn't reach their ends.
Inputs may be any that keep to these rules, and one draw needn't show every extreme that they name: `block_rows`: in each panel the live slots name distinct pairs of block row and block column; ids in the other slots lie in the same ranges and mean nothing. `panel_counts`: some panel has all 128 slots live.
All inputs are finite; a program needn't handle non-finite values.
Results may differ from the reference program's by a relative error of at most 0.02.
Values may be sent and summed in bfloat16 or wider, within the bound.
No kernel may reach another device: no remote copies, remote signals or barrier semaphores. Data moves between devices by JAX's collectives and lax.ppermute only.
A program may use at most 64 MiB of HBM per device.

```python
import jax
import jax.numpy as jnp
from jax import lax

D = 6144
FF = 49152
BLK = 64
TOK_R = 128
TOKENS = 4096
NPANEL = 16
CAP = 128
BCP = 48
NBR = 96
N_ROW = 32


def pattern_lists(key):
    base_rows = jax.random.randint(jax.random.fold_in(key, 17), (NPANEL, BCP), 0, NBR)
    flat_index = jnp.arange(NPANEL * BCP).reshape(NPANEL, BCP)
    base_rows = jnp.where(flat_index == 0, NBR - 1, jnp.where(flat_index == 1, 0, base_rows))
    slot_index = jnp.arange(CAP)
    levels = slot_index // BCP
    column = slot_index % BCP
    offsets = jnp.where(levels == 0, 0, jnp.left_shift(jnp.ones_like(levels), jnp.maximum(levels - 1, 0)))
    row_ids = (base_rows[:, column] + offsets[None, :]) % NBR
    col_ids = jnp.broadcast_to(column[None, :], (NPANEL, CAP))
    scores = jax.random.randint(jax.random.fold_in(key, 29), (NPANEL, CAP), 0, 1 << 20) * CAP + slot_index[None, :]
    ranking = jnp.argsort(scores, axis=1, stable=True)
    shuffled_rows = jnp.take_along_axis(row_ids, ranking, axis=1).astype(jnp.int32)
    shuffled_cols = jnp.take_along_axis(col_ids, ranking, axis=1).astype(jnp.int32)
    return (shuffled_rows, shuffled_cols)


def draw_block_rows(key, part):
    return pattern_lists(key)[0]


def draw_block_columns(key, part):
    return pattern_lists(key)[1]


def draw_panel_counts(key, part):
    values = jax.random.randint(jax.random.fold_in(key, 41), (NPANEL,), CAP // 8, CAP + 1)
    fullest = jax.random.randint(jax.random.fold_in(key, 43), (), 0, NPANEL)
    return jnp.where(jnp.arange(NPANEL) == fullest, CAP, values).astype(jnp.int32)


def block_levels(stream_key, extent, pieces, low, top_value):
    def one(dim, blocks):
        draws = jax.random.uniform(jax.random.fold_in(jax.random.fold_in(stream_key, 6), dim), (blocks,), jnp.float32, low / len(pieces), top_value / len(pieces))
        return jnp.repeat(jnp.exp(draws), extent[dim] // blocks).reshape((-1,) + (1,) * (len(extent) - dim - 1))

    loudness = one(*pieces[0])
    for cut in pieces[1:]:
        loudness = loudness * one(*cut)
    return loudness


def bell_draw(key, extent, scale, bound, pieces=(), kind=jnp.bfloat16):
    values = scale * jax.random.normal(key, extent, jnp.float32)
    if pieces:
        values = values * block_levels(key, extent, pieces, -0.22, 0.18)
    return jnp.clip(values, -bound, bound).astype(kind)


def setup_inputs(seed: int = 0) -> dict:
    key_list = jax.random.split(jax.random.key(seed), 7)
    return {
        "tokens": bell_draw(key_list[0], (TOKENS, D), 1.0, 6.0, ((0, 32), (1, 16))),
        "weight_blocks": bell_draw(key_list[1], (NPANEL, CAP, BLK * BLK), (4 * BLK) ** -0.5, 0.375, ((0, 16), (1, 32))),
        "block_rows": draw_block_rows(jax.random.fold_in(key_list[6], 71), 0),
        "block_columns": draw_block_columns(jax.random.fold_in(key_list[6], 71), 0),
        "panel_counts": draw_panel_counts(jax.random.fold_in(key_list[6], 71), 0),
        "hidden_grad": bell_draw(key_list[5], (TOKENS, FF), 0.2, 1.1953125, ((0, 32), (1, 16))),
    }


root_two_pi = 0.7978845608028654
cubic_term = 0.044715


def gelu_value(pre_act):
    inner = root_two_pi * (pre_act + cubic_term * pre_act * pre_act * pre_act)
    return 0.5 * pre_act * (1.0 + jnp.tanh(inner))


def gelu_slope(pre_act):
    inner = root_two_pi * (pre_act + cubic_term * pre_act * pre_act * pre_act)
    tangent = jnp.tanh(inner)
    return 0.5 * (1.0 + tangent) + 0.5 * pre_act * (1.0 - tangent * tangent) * root_two_pi * (1.0 + 3.0 * cubic_term * pre_act * pre_act)


def reference(tokens, weight_blocks, block_rows, block_columns, panel_counts, hidden_grad):
    token_blocks = tokens.reshape(TOKENS, NBR, BLK)
    grad_panels = hidden_grad.reshape(TOKENS, NPANEL, BCP, BLK)
    slot_index = jnp.arange(CAP, dtype=jnp.int32)

    def panel_step(input_total, panel_index):
        live_slots = slot_index < panel_counts[panel_index]
        blocks = weight_blocks[panel_index].reshape(CAP, BLK, BLK)
        blocks = jnp.where(live_slots[:, None, None], blocks, jnp.zeros_like(blocks)).astype(jnp.float32)
        rows_here = block_rows[panel_index]
        cols_here = block_columns[panel_index]
        picked = jnp.take(token_blocks, rows_here, axis=1).astype(jnp.float32)
        products = jnp.einsum("tsa,sab->stb", picked, blocks)
        pre_act = jax.ops.segment_sum(products, cols_here, num_segments=BCP).transpose(1, 0, 2)
        hidden_panel = gelu_value(pre_act).astype(jnp.bfloat16)
        upstream = lax.dynamic_index_in_dim(grad_panels, panel_index, 1, keepdims=False).astype(jnp.float32)
        grad_blocks = (upstream * gelu_slope(pre_act)).astype(jnp.bfloat16)
        picked_grad = jnp.take(grad_blocks, cols_here, axis=1).astype(jnp.float32)
        backward = jnp.einsum("tsb,sab->sta", picked_grad, blocks)
        input_part = jax.ops.segment_sum(backward, rows_here, num_segments=NBR).transpose(1, 0, 2).reshape(TOKENS, D)
        input_part = lax.optimization_barrier(input_part.astype(jnp.bfloat16)).astype(jnp.float32)
        grouped = jnp.einsum("rtsa,rtsb->rsab", picked.reshape(N_ROW, TOK_R, CAP, BLK), picked_grad.reshape(N_ROW, TOK_R, CAP, BLK))
        grouped = lax.optimization_barrier(grouped.astype(jnp.bfloat16)).astype(jnp.float32)
        weight_part = jnp.sum(grouped, axis=0)
        weight_part = jnp.where(live_slots[:, None, None], weight_part, jnp.zeros_like(weight_part))
        weight_part = weight_part.reshape(CAP, BLK * BLK).astype(jnp.bfloat16)
        return input_total + input_part, (hidden_panel, weight_part)

    input_total, outputs = lax.scan(panel_step, jnp.zeros((TOKENS, D), jnp.float32), jnp.arange(NPANEL, dtype=jnp.int32))
    hidden_panels, weight_grad = outputs
    hidden = hidden_panels.transpose(1, 0, 2, 3).reshape(TOKENS, FF)
    return hidden, input_total.astype(jnp.bfloat16), weight_grad
```

```python
import jax
import jax.numpy as jnp
from jax import lax
from jax.experimental import pallas as pl
from jax.experimental.pallas import tpu as pltpu
from jax.sharding import PartitionSpec as P

root_two_pi = 0.7978845608028654
cubic_term = 0.044715
BF = jnp.bfloat16
F32 = jnp.float32
BLK = 64
NT = (((1,), (1,)), ((), ()))
TN = (((0,), (0,)), ((), ()))
SEEDS = (0, 5, -5)
ABOVE1 = (1, 6, -4)
BELOW1 = (-1, 4, -6)
ABOVE2 = (2, 7, -3)
BELOW2 = (-2, 3, -7)


def dot(a, b, dims=(((1,), (0,)), ((), ()))):
    return lax.dot_general(a, b, dims, preferred_element_type=F32)


def eye():
    i = lax.broadcasted_iota(jnp.int32, (128, 128), 0)
    j = lax.broadcasted_iota(jnp.int32, (128, 128), 1)
    return (i == j).astype(BF)


def forward_kernel(
    ids, weights, s0, a1, b1, a2, b2, e8, upstream, hidden, grad, whole, pre
):
    for piece, offsets in ((s0, SEEDS), (a1, ABOVE1), (b1, BELOW1), (a2, ABOVE2), (b2, BELOW2), (e8, (8,))):
        for k, offset in enumerate(offsets):
            at = offset % 16 * 6
            whole[at : at + 6] = piece[k].reshape(6, BLK, 128)
    pre[...] = jnp.zeros_like(pre)

    def some_slots(g, carry):
        for q in range(4):
            d = g * 4 + q
            for j in range(4):
                half = (j % 2) * BLK
                block = weights[d, (j // 2) * BLK : (j // 2 + 1) * BLK, half : half + BLK]
                row, column = ids[d, j], ids[d, 4 + j]
                pre[column] += dot(block, whole[row], TN)
        return carry

    lax.fori_loop(0, 8, some_slots, 0)

    unit = eye()

    def some_columns(g, carry):
        at = pl.multiple_of(g * 128, 128)
        v = pre[pl.ds(g * 2, 2)].reshape(128, 128)
        tangent = jnp.tanh(root_two_pi * (v + cubic_term * v * v * v))
        value = 0.5 * v * (1.0 + tangent)
        slope = 0.5 * (1.0 + tangent) + 0.5 * v * (1.0 - tangent * tangent) * root_two_pi * (
            1.0 + 3.0 * cubic_term * v * v
        )
        turned = dot(unit, upstream[:, pl.ds(at, 128)], NT)
        grad[pl.ds(g * 2, 2)] = (turned * slope).astype(BF).reshape(2, BLK, 128)
        hidden[:, pl.ds(at, 128)] = dot(unit, value.astype(BF), NT).astype(BF)
        return carry

    lax.fori_loop(0, 24, some_columns, 0)


def input_kernel(ids, weights, grad, v0, a1, b1, a2, b2, e8, total):
    total[...] = jnp.zeros_like(total)

    def some_slots(g, carry):
        for q in range(4):
            d = g * 4 + q
            for j in range(4):
                half = (j % 2) * BLK
                block = weights[d, (j // 2) * BLK : (j // 2 + 1) * BLK, half : half + BLK]
                row, column = ids[d, j], ids[d, 4 + j]
                total[row] += dot(block, grad[column])
        return carry

    lax.fori_loop(0, 8, some_slots, 0)
    for piece, offsets in ((v0, SEEDS), (a1, ABOVE1), (b1, BELOW1), (a2, ABOVE2), (b2, BELOW2), (e8, (8,))):
        for k, offset in enumerate(offsets):
            at = offset % 16 * 6
            piece[k] = total[at : at + 6].reshape(384, 128).astype(BF)


def weight_kernel(ids, whole, grad, out):
    def some_slots(g, carry):
        for q in range(4):
            d = g * 4 + q
            for j in range(4):
                half = (j % 2) * BLK
                row, column = ids[d, j], ids[d, 4 + j]
                block = dot(whole[row], grad[column], NT).astype(BF)
                out[d, (j // 2) * BLK : (j // 2 + 1) * BLK, half : half + BLK] = block
        return carry

    lax.fori_loop(0, 8, some_slots, 0)


SM = pl.BlockSpec(memory_space=pltpu.SMEM)
VM = pl.BlockSpec(memory_space=pltpu.VMEM)
MIB = 1 << 20


def shape(*dims):
    return jax.ShapeDtypeStruct(dims, BF)


def call(kernel, outs, n_in, scratch, flops, limit):
    return pl.pallas_call(
        kernel,
        out_shape=outs,
        in_specs=[SM] + [VM] * (n_in - 1),
        out_specs=jax.tree.map(lambda _: VM, outs),
        scratch_shapes=scratch,
        compiler_params=pltpu.CompilerParams(vmem_limit_bytes=limit * MIB),
        cost_estimate=pl.CostEstimate(flops=flops, bytes_accessed=6 * MIB, transcendentals=0),
    )


def on_device(tokens, weight_blocks, block_rows, block_columns, panel_counts, hidden_grad):
    n_col, n_row = lax.axis_size("col"), lax.axis_size("row")
    me_col, me_row = lax.axis_index("col"), lax.axis_index("row")

    def shift(a, by):
        return lax.ppermute(a, "col", [(i, (i + by) % n_col) for i in range(n_col)])

    mine = tokens.T
    far = jnp.stack([mine, shift(mine, -5), shift(mine, 5)])

    slot = me_row * 4 + jnp.arange(4, dtype=jnp.int32)
    live = slot < panel_counts[0]
    blocks = jnp.where(live[:, None, None], weight_blocks[0].reshape(4, BLK, BLK), 0)
    blocks = blocks.reshape(2, 2, BLK, BLK).transpose(0, 2, 1, 3).reshape(128, 128)
    named = jnp.concatenate([block_rows[0], block_columns[0]]).astype(BF)
    named = jnp.pad(named[None, :], ((0, 15), (0, 120)))
    parcel = jnp.broadcast_to(jnp.concatenate([blocks, named])[None], (n_row, 144, 128))
    parcels = lax.all_to_all(parcel, "row", 0, 0, tiled=True)
    ids = parcels[:, 128, :8].astype(jnp.int32)
    rows = (ids[:, :4] + (96 - 6 * me_col)) % 96
    ids = jnp.concatenate([rows, ids[:, 4:]], axis=1)

    above1, below1 = shift(far, -1), shift(far, 1)
    above2, below2 = shift(above1, -1), shift(below1, 1)
    eight = shift(above1[1:2], -2)

    hidden, grad, whole = call(
        forward_kernel,
        (shape(128, 3072), shape(48, BLK, 128), shape(96, BLK, 128)),
        9,
        [pltpu.VMEM((48, BLK, 128), F32)],
        400_000_000,
        24,
    )(ids, parcels, far, above1, below1, above2, below2, eight, hidden_grad)

    three = shape(3, 384, 128)
    v0, a1, b1, a2, b2, e8 = call(
        input_kernel,
        (three, three, three, three, three, shape(1, 384, 128)),
        3,
        [pltpu.VMEM((96, BLK, 128), F32)],
        300_000_000,
        24,
    )(ids, parcels, grad)

    def plus(a, *more):
        total = a.astype(F32)
        for m in more:
            total = total + m.astype(F32)
        return total.astype(BF)

    from8 = shift(e8, 2)
    up, down = shift(a2, 1), shift(b2, -1)
    a1 = plus(a1, up, jnp.pad(from8, ((1, 1), (0, 0), (0, 0))))
    b1 = plus(b1, down)

    terms = call(weight_kernel, shape(n_row, 128, 128), 3, [], 300_000_000, 16)(ids, whole, grad)
    back = lax.all_to_all(terms, "row", 0, 0, tiled=True)

    v0 = plus(v0, shift(a1, 1), shift(b1, -1))
    own = plus(v0[0], shift(v0[1], 5), shift(v0[2], -5))
    input_grad = own.T

    sums = jnp.sum(back.astype(F32), axis=0).astype(BF)
    sums = sums.reshape(2, BLK, 2, BLK).transpose(0, 2, 1, 3).reshape(4, BLK * BLK)
    weight_grad = jnp.where(live[:, None], sums, 0)[None]
    return hidden, input_grad, weight_grad


def solution(mesh):
    placed = (
        P("row", "col"),
        P("col", "row", None),
        P("col", "row"),
        P("col", "row"),
        P("col"),
        P("row", "col"),
    )
    return jax.shard_map(
        on_device,
        mesh=mesh,
        in_specs=placed,
        out_specs=(P("row", "col"), P("row", "col"), P("col", "row", None)),
        check_vma=False,
    )
```

```python
import jax
import jax.numpy as jnp
from jax import lax
from jax.experimental import pallas as pl
from jax.experimental.pallas import tpu as pltpu
from jax.sharding import PartitionSpec as P

root_two_pi = 0.7978845608028654
cubic_term = 0.044715
BF = jnp.bfloat16
F32 = jnp.float32
BLK = 64
NT = (((1,), (1,)), ((), ()))
TN = (((0,), (0,)), ((), ()))
SEEDS = (0, 5, -5)
ABOVE1 = (1, 6, -4)
BELOW1 = (-1, 4, -6)
ABOVE2 = (2, 7, -3)
BELOW2 = (-2, 3, -7)


def dot(a, b, dims=(((1,), (0,)), ((), ()))):
    return lax.dot_general(a, b, dims, preferred_element_type=F32)


def eye():
    i = lax.broadcasted_iota(jnp.int32, (128, 128), 0)
    j = lax.broadcasted_iota(jnp.int32, (128, 128), 1)
    return (i == j).astype(BF)


def forward_kernel(
    ids, weights, s0, a1, b1, a2, b2, e8, upstream, hidden, grad, whole, pre
):
    for piece, offsets in ((s0, SEEDS), (a1, ABOVE1), (b1, BELOW1), (a2, ABOVE2), (b2, BELOW2), (e8, (8,))):
        for k, offset in enumerate(offsets):
            at = offset % 16 * 6
            whole[at : at + 6] = piece[k].reshape(6, BLK, 128)
    pre[...] = jnp.zeros_like(pre)

    def some_slots(g, carry):
        for q in range(4):
            d = g * 4 + q
            for j in range(4):
                half = (j % 2) * BLK
                block = weights[d, (j // 2) * BLK : (j // 2 + 1) * BLK, half : half + BLK]
                row, column = ids[d, j], ids[d, 4 + j]
                pre[column] += dot(block, whole[row], TN)
        return carry

    lax.fori_loop(0, 8, some_slots, 0)

    unit = eye()

    def some_columns(g, carry):
        at = pl.multiple_of(g * 128, 128)
        v = pre[pl.ds(g * 2, 2)].reshape(128, 128)
        tangent = jnp.tanh(root_two_pi * (v + cubic_term * v * v * v))
        value = 0.5 * v * (1.0 + tangent)
        slope = 0.5 * (1.0 + tangent) + 0.5 * v * (1.0 - tangent * tangent) * root_two_pi * (
            1.0 + 3.0 * cubic_term * v * v
        )
        turned = dot(unit, upstream[:, pl.ds(at, 128)], NT)
        grad[pl.ds(g * 2, 2)] = (turned * slope).astype(BF).reshape(2, BLK, 128)
        hidden[:, pl.ds(at, 128)] = dot(unit, value.astype(BF), NT).astype(BF)
        return carry

    lax.fori_loop(0, 24, some_columns, 0)


def input_kernel(ids, weights, grad, out, total):
    total[...] = jnp.zeros_like(total)

    def some_slots(g, carry):
        for q in range(4):
            d = g * 4 + q
            for j in range(4):
                half = (j % 2) * BLK
                block = weights[d, (j // 2) * BLK : (j // 2 + 1) * BLK, half : half + BLK]
                row, column = ids[d, 8 + j], ids[d, 4 + j]
                total[row] += dot(block, grad[column])
        return carry

    lax.fori_loop(0, 8, some_slots, 0)
    for o in range(16):
        out[400 * o : 400 * o + 384] = total[6 * o : 6 * o + 6].reshape(384, 128).astype(BF)
        if o < 15:
            out[400 * o + 384 : 400 * o + 400] = jnp.zeros((16, 128), BF)


def weight_kernel(ids, whole, grad, out):
    def some_slots(g, carry):
        for q in range(4):
            d = g * 4 + q
            for j in range(4):
                half = (j % 2) * BLK
                row, column = ids[d, j], ids[d, 4 + j]
                block = dot(whole[row], grad[column], NT).astype(BF)
                out[d, (j // 2) * BLK : (j // 2 + 1) * BLK, half : half + BLK] = block
        return carry

    lax.fori_loop(0, 8, some_slots, 0)


SM = pl.BlockSpec(memory_space=pltpu.SMEM)
VM = pl.BlockSpec(memory_space=pltpu.VMEM)
MIB = 1 << 20


def shape(*dims):
    return jax.ShapeDtypeStruct(dims, BF)


def call(kernel, outs, n_in, scratch, flops, limit):
    return pl.pallas_call(
        kernel,
        out_shape=outs,
        in_specs=[SM] + [VM] * (n_in - 1),
        out_specs=jax.tree.map(lambda _: VM, outs),
        scratch_shapes=scratch,
        compiler_params=pltpu.CompilerParams(vmem_limit_bytes=limit * MIB),
        cost_estimate=pl.CostEstimate(flops=flops, bytes_accessed=6 * MIB, transcendentals=0),
    )


def on_device(tokens, weight_blocks, block_rows, block_columns, panel_counts, hidden_grad):
    n_col, n_row = lax.axis_size("col"), lax.axis_size("row")
    me_col, me_row = lax.axis_index("col"), lax.axis_index("row")

    def shift(a, by):
        return lax.ppermute(a, "col", [(i, (i + by) % n_col) for i in range(n_col)])

    mine = tokens.T
    far = jnp.stack([mine, shift(mine, -5), shift(mine, 5)])

    slot = me_row * 4 + jnp.arange(4, dtype=jnp.int32)
    live = slot < panel_counts[0]
    blocks = jnp.where(live[:, None, None], weight_blocks[0].reshape(4, BLK, BLK), 0)
    blocks = blocks.reshape(2, 2, BLK, BLK).transpose(0, 2, 1, 3).reshape(128, 128)
    named = jnp.concatenate([block_rows[0], block_columns[0]]).astype(BF)
    named = jnp.pad(named[None, :], ((0, 15), (0, 120)))
    parcel = jnp.broadcast_to(jnp.concatenate([blocks, named])[None], (n_row, 144, 128))
    parcels = lax.all_to_all(parcel, "row", 0, 0, tiled=True)
    ids = parcels[:, 128, :8].astype(jnp.int32)
    rows = (ids[:, :4] + (96 - 6 * me_col)) % 96
    ids = jnp.concatenate([rows, ids[:, 4:], ids[:, :4]], axis=1)

    above1, below1 = shift(far, -1), shift(far, 1)
    above2, below2 = shift(above1, -1), shift(below1, 1)
    eight = shift(above1[1:2], -2)

    hidden, grad, whole = call(
        forward_kernel,
        (shape(128, 3072), shape(48, BLK, 128), shape(96, BLK, 128)),
        9,
        [pltpu.VMEM((48, BLK, 128), F32)],
        400_000_000,
        24,
    )(ids, parcels, far, above1, below1, above2, below2, eight, hidden_grad)

    terms = call(weight_kernel, shape(n_row, 128, 128), 3, [], 300_000_000, 16)(ids, whole, grad)
    back = lax.all_to_all(terms, "row", 0, 0, tiled=True)

    part = call(
        input_kernel, shape(6384, 128), 3, [pltpu.VMEM((96, BLK, 128), F32)], 300_000_000, 24
    )(ids, parcels, grad)
    own = lax.optimization_barrier(lax.psum_scatter(part, "col", scatter_dimension=0, tiled=True))
    input_grad = lax.dynamic_slice_in_dim(own, me_col, 384, 0).T

    sums = jnp.sum(back.astype(F32), axis=0).astype(BF)
    sums = sums.reshape(2, BLK, 2, BLK).transpose(0, 2, 1, 3).reshape(4, BLK * BLK)
    weight_grad = jnp.where(live[:, None], sums, 0)[None]
    return hidden, input_grad, weight_grad


def solution(mesh):
    placed = (
        P("row", "col"),
        P("col", "row", None),
        P("col", "row"),
        P("col", "row"),
        P("col"),
        P("row", "col"),
    )
    return jax.shard_map(
        on_device,
        mesh=mesh,
        in_specs=placed,
        out_specs=(P("row", "col"), P("row", "col"), P("col", "row", None)),
        check_vma=False,
    )
```

```python
import jax
import jax.numpy as jnp
from jax import lax
from jax.experimental import pallas as pl
from jax.experimental.pallas import tpu as pltpu
from jax.sharding import Mesh
from jax.sharding import PartitionSpec as P

root_two_pi = 0.7978845608028654
cubic_term = 0.044715
BF = jnp.bfloat16
F32 = jnp.float32
BLK = 64
NT = (((1,), (1,)), ((), ()))
TN = (((0,), (0,)), ((), ()))
COL = ("half", "side")


def dot(a, b, dims=(((1,), (0,)), ((), ()))):
    return lax.dot_general(a, b, dims, preferred_element_type=F32)


def eye():
    i = lax.broadcasted_iota(jnp.int32, (128, 128), 0)
    j = lax.broadcasted_iota(jnp.int32, (128, 128), 1)
    return (i == j).astype(BF)


def forward_kernel(
    ids, weights, same, other_low, other_high, upstream, hidden, grad, whole, pre
):
    whole[:48] = same[...].reshape(48, BLK, 128)
    whole[48:72] = other_low[...].reshape(24, BLK, 128)
    whole[72:] = other_high[...].reshape(24, BLK, 128)
    pre[...] = jnp.zeros_like(pre)

    def some_slots(g, carry):
        for q in range(4):
            d = g * 4 + q
            for j in range(4):
                half = (j % 2) * BLK
                block = weights[d, (j // 2) * BLK : (j // 2 + 1) * BLK, half : half + BLK]
                row, column = ids[d, j], ids[d, 4 + j]
                pre[column] += dot(block, whole[row], TN)
        return carry

    lax.fori_loop(0, 8, some_slots, 0)

    unit = eye()

    def some_columns(g, carry):
        at = pl.multiple_of(g * 128, 128)
        v = pre[pl.ds(g * 2, 2)].reshape(128, 128)
        tangent = jnp.tanh(root_two_pi * (v + cubic_term * v * v * v))
        value = 0.5 * v * (1.0 + tangent)
        slope = 0.5 * (1.0 + tangent) + 0.5 * v * (1.0 - tangent * tangent) * root_two_pi * (
            1.0 + 3.0 * cubic_term * v * v
        )
        turned = dot(unit, upstream[:, pl.ds(at, 128)], NT)
        grad[pl.ds(g * 2, 2)] = (turned * slope).astype(BF).reshape(2, BLK, 128)
        hidden[:, pl.ds(at, 128)] = dot(unit, value.astype(BF), NT).astype(BF)
        return carry

    lax.fori_loop(0, 24, some_columns, 0)


def input_kernel(ids, weights, grad, out, total):
    total[...] = jnp.zeros_like(total)

    def some_slots(g, carry):
        for q in range(4):
            d = g * 4 + q
            for j in range(4):
                half = (j % 2) * BLK
                block = weights[d, (j // 2) * BLK : (j // 2 + 1) * BLK, half : half + BLK]
                row, column = ids[d, 8 + j], ids[d, 4 + j]
                total[row] += dot(block, grad[column])
        return carry

    lax.fori_loop(0, 8, some_slots, 0)
    for o in range(16):
        out[400 * o : 400 * o + 384] = total[6 * o : 6 * o + 6].reshape(384, 128).astype(BF)
        if o < 15:
            out[400 * o + 384 : 400 * o + 400] = jnp.zeros((16, 128), BF)


def weight_kernel(ids, whole, grad, out):
    def some_slots(g, carry):
        for q in range(4):
            d = g * 4 + q
            for j in range(4):
                half = (j % 2) * BLK
                row, column = ids[d, j], ids[d, 4 + j]
                block = dot(whole[row], grad[column], NT).astype(BF)
                out[d, (j // 2) * BLK : (j // 2 + 1) * BLK, half : half + BLK] = block
        return carry

    lax.fori_loop(0, 8, some_slots, 0)


SM = pl.BlockSpec(memory_space=pltpu.SMEM)
VM = pl.BlockSpec(memory_space=pltpu.VMEM)
MIB = 1 << 20


def shape(*dims):
    return jax.ShapeDtypeStruct(dims, BF)


def call(kernel, outs, n_in, scratch, flops, limit):
    return pl.pallas_call(
        kernel,
        out_shape=outs,
        in_specs=[SM] + [VM] * (n_in - 1),
        out_specs=jax.tree.map(lambda _: VM, outs),
        scratch_shapes=scratch,
        compiler_params=pltpu.CompilerParams(vmem_limit_bytes=limit * MIB),
        cost_estimate=pl.CostEstimate(flops=flops, bytes_accessed=6 * MIB, transcendentals=0),
    )


def on_device(tokens, weight_blocks, block_rows, block_columns, panel_counts, hidden_grad):
    n_row, n_col = lax.axis_size("row"), lax.axis_size(COL)
    me_row, me_col, me_side = lax.axis_index("row"), lax.axis_index(COL), lax.axis_index("side")

    def shift(a, by):
        return lax.ppermute(a, COL, [(i, (i + by) % n_col) for i in range(n_col)])

    slot = me_row * 4 + jnp.arange(4, dtype=jnp.int32)
    live = slot < panel_counts[0]
    blocks = jnp.where(live[:, None, None], weight_blocks[0].reshape(4, BLK, BLK), 0)
    blocks = blocks.reshape(2, 2, BLK, BLK).transpose(0, 2, 1, 3).reshape(128, 128)
    named = jnp.concatenate([block_rows[0], block_columns[0]]).astype(BF)
    named = jnp.pad(named[None, :], ((0, 15), (0, 120)))
    parcel = jnp.broadcast_to(jnp.concatenate([blocks, named])[None], (n_row, 144, 128))
    parcels = lax.all_to_all(parcel, "row", 0, 0, tiled=True)
    ids = parcels[:, 128, :8].astype(jnp.int32)
    owner = ids[:, :4] // 6
    rows = jnp.where(owner % 2 == me_side, 0, 48) + owner // 2 * 6 + ids[:, :4] % 6
    ids = jnp.concatenate([rows, ids[:, 4:], ids[:, :4]], axis=1)

    same = lax.all_gather(tokens.T, "half", axis=0, tiled=True)
    middle = same.shape[0] // 2
    other_low, other_high = shift(same[:middle], 1), shift(same[middle:], -1)

    hidden, grad, whole = call(
        forward_kernel,
        (shape(128, 3072), shape(48, BLK, 128), shape(96, BLK, 128)),
        6,
        [pltpu.VMEM((48, BLK, 128), F32)],
        400_000_000,
        24,
    )(ids, parcels, same, other_low, other_high, hidden_grad)

    terms = call(weight_kernel, shape(n_row, 128, 128), 3, [], 300_000_000, 16)(ids, whole, grad)
    back = lax.all_to_all(terms, "row", 0, 0, tiled=True)

    part = call(
        input_kernel, shape(6384, 128), 3, [pltpu.VMEM((96, BLK, 128), F32)], 300_000_000, 24
    )(ids, parcels, grad)
    own = lax.optimization_barrier(lax.psum_scatter(part, COL, scatter_dimension=0, tiled=True))
    input_grad = lax.dynamic_slice_in_dim(own, me_col, 384, 0).T

    sums = jnp.sum(back.astype(F32), axis=0).astype(BF)
    sums = sums.reshape(2, BLK, 2, BLK).transpose(0, 2, 1, 3).reshape(4, BLK * BLK)
    weight_grad = jnp.where(live[:, None], sums, 0)[None]
    return hidden, input_grad, weight_grad


def solution(mesh):
    n_row, n_col = mesh.devices.shape
    fine = Mesh(mesh.devices.reshape(n_row, n_col // 2, 2), ("row", *COL))
    placed = (
        P("row", COL),
        P(COL, "row", None),
        P(COL, "row"),
        P(COL, "row"),
        P(COL),
        P("row", COL),
    )
    return jax.shard_map(
        on_device,
        mesh=fine,
        in_specs=placed,
        out_specs=(P("row", COL), P("row", COL), P(COL, "row", None)),
        check_vma=False,
    )
```

```python
import jax
import jax.numpy as jnp
from jax import lax
from jax.experimental import pallas as pl
from jax.experimental.pallas import tpu as pltpu
from jax.sharding import Mesh
from jax.sharding import PartitionSpec as P

root_two_pi = 0.7978845608028654
cubic_term = 0.044715
BF = jnp.bfloat16
F32 = jnp.float32
BLK = 64
NN = (((1,), (0,)), ((), ()))
NT = (((1,), (1,)), ((), ()))
TN = (((0,), (0,)), ((), ()))
COL = ("half", "side")
SM = pl.BlockSpec(memory_space=pltpu.SMEM)
VM = pl.BlockSpec(memory_space=pltpu.VMEM)
MIB = 1 << 20


def dot(a, b, dims=NN):
    return lax.dot_general(a, b, dims, preferred_element_type=F32)


def picker(parted):
    i = lax.broadcasted_iota(jnp.int32, (128, 128), 0)
    j = lax.broadcasted_iota(jnp.int32, (128, 128), 1)
    place = i // 64 * 64 + i % 32 * 2 + i % 64 // 32
    return ((place if parted else i) == j).astype(BF)


def prep_kernel(rows, columns, count, first, blocks, tokens, parcels, turned, spread):
    for i in range(32):
        spread[pl.ds(i, 4, stride=32), :] = blocks[0, :, i * 128 : (i + 1) * 128].astype(F32)
    slot = first[0] + lax.broadcasted_iota(jnp.int32, (128, 128), 0) // 32
    parcels[0, :128] = jnp.where(slot < count[0], spread[...], 0.0).astype(BF)
    lane = lax.broadcasted_iota(jnp.int32, (16, 128), 1)
    named = jnp.zeros((16, 128), jnp.int32)
    for j in range(4):
        named = jnp.where(lane == j, rows[0, j], named)
        named = jnp.where(lane == 4 + j, columns[0, j], named)
    parcels[0, 128:] = named.astype(F32).astype(BF)

    def again(d, carry):
        parcels[d] = parcels[0]
        return carry

    lax.fori_loop(1, parcels.shape[0], again, 0)
    parted = picker(True)
    for k in range(3):
        at = k * 128
        turned[at : at + 128] = dot(parted, tokens[:, at : at + 128], NT).astype(BF)


def main_kernel(
    ids, weights, same, other_low, other_high, upstream, hidden, part, terms, whole, pre, grad, total
):
    whole[:48] = same[...].reshape(48, BLK, 128)
    whole[48:72] = other_low[...].reshape(24, BLK, 128)
    whole[72:] = other_high[...].reshape(24, BLK, 128)
    pre[...] = jnp.zeros_like(pre)
    total[...] = jnp.zeros_like(total)

    def slots(visit):
        def some(g, carry):
            for q in range(8):
                for j in range(4):
                    visit(g * 8 + q, j)
            return carry

        lax.fori_loop(0, 4, some, 0)

    def block(d, j):
        lines = weights[d, j * 32 : (j + 1) * 32]
        return jnp.concatenate([lines[:, :BLK], lines[:, BLK:]], axis=0)

    def forward(d, j):
        pre[ids[d, 4 + j]] += dot(block(d, j), whole[ids[d, j]], TN)

    slots(forward)
    unit = picker(False)

    def some_columns(g, carry):
        at = pl.multiple_of(g * 128, 128)
        v = pre[pl.ds(g * 2, 2)].reshape(128, 128)
        tangent = jnp.tanh(root_two_pi * (v + cubic_term * v * v * v))
        value = 0.5 * v * (1.0 + tangent)
        slope = 0.5 * (1.0 + tangent) + 0.5 * v * (1.0 - tangent * tangent) * root_two_pi * (
            1.0 + 3.0 * cubic_term * v * v
        )
        turned = dot(unit, upstream[:, pl.ds(at, 128)], NT)
        grad[pl.ds(g * 2, 2)] = (turned * slope).astype(BF).reshape(2, BLK, 128)
        hidden[:, pl.ds(at, 128)] = dot(unit, value.astype(BF), NT).astype(BF)
        return carry

    lax.fori_loop(0, 24, some_columns, 0, unroll=4)

    def weight(d, j):
        product = dot(whole[ids[d, j]], grad[ids[d, 4 + j]], NT).astype(BF)
        terms[d, j * 32 : (j + 1) * 32] = jnp.concatenate([product[:32], product[32:]], axis=1)

    slots(weight)

    def backward(d, j):
        total[ids[d, 8 + j]] += dot(block(d, j), grad[ids[d, 4 + j]])

    slots(backward)
    for o in range(16):
        part[400 * o : 400 * o + 384] = total[6 * o : 6 * o + 6].reshape(384, 128).astype(BF)
        if o < 15:
            part[400 * o + 384 : 400 * o + 400] = jnp.zeros((16, 128), BF)


def weight_end_kernel(count, first, terms, out, total):
    def some(d, kept):
        return kept + terms[d].astype(F32)

    kept = lax.fori_loop(1, terms.shape[0], some, terms[0].astype(F32))
    slot = first[0] + lax.broadcasted_iota(jnp.int32, (128, 128), 0) // 32
    total[...] = jnp.where(slot < count[0], kept, 0.0)
    for i in range(32):
        out[0, :, i * 128 : (i + 1) * 128] = total[pl.ds(i, 4, stride=32), :].astype(BF)


def input_end_kernel(own, out):
    parted = picker(True)
    for k in range(3):
        at = k * 128
        out[:, at : at + 128] = dot(own[at : at + 128], parted, TN).astype(BF)


def shape(*dims):
    return jax.ShapeDtypeStruct(dims, BF)


def call(kernel, outs, n_scalar, n_array, scratch, flops, limit):
    return pl.pallas_call(
        kernel,
        out_shape=outs,
        in_specs=[SM] * n_scalar + [VM] * n_array,
        out_specs=jax.tree.map(lambda _: VM, outs),
        scratch_shapes=scratch,
        compiler_params=pltpu.CompilerParams(vmem_limit_bytes=limit * MIB),
        cost_estimate=pl.CostEstimate(flops=flops, bytes_accessed=2 * MIB, transcendentals=0),
    )


def on_device(tokens, weight_blocks, block_rows, block_columns, panel_counts, hidden_grad):
    n_row, n_col = lax.axis_size("row"), lax.axis_size(COL)
    me_row, me_col, me_side = lax.axis_index("row"), lax.axis_index(COL), lax.axis_index("side")
    first = (me_row * 4).reshape(1)

    def shift(a, by):
        return lax.ppermute(a, COL, [(i, (i + by) % n_col) for i in range(n_col)])

    parcels, turned = call(
        prep_kernel,
        (shape(n_row, 144, 128), shape(384, 128)),
        4,
        2,
        [pltpu.VMEM((128, 128), F32)],
        10_000_000,
        8,
    )(block_rows, block_columns, panel_counts, first, weight_blocks, tokens)
    parcels = lax.all_to_all(parcels, "row", 0, 0, tiled=True)
    ids = parcels[:, 128, :8].astype(jnp.int32)
    owner = ids[:, :4] // 6
    rows = jnp.where(owner % 2 == me_side, 0, 48) + owner // 2 * 6 + ids[:, :4] % 6
    ids = jnp.concatenate([rows, ids[:, 4:], ids[:, :4]], axis=1)

    same = lax.all_gather(turned, "half", axis=0, tiled=True)
    middle = same.shape[0] // 2
    other_low, other_high = shift(same[:middle], 1), shift(same[middle:], -1)

    hidden, part, terms = call(
        main_kernel,
        (shape(128, 3072), shape(6384, 128), shape(n_row, 128, 128)),
        1,
        5,
        [
            pltpu.VMEM((96, BLK, 128), BF),
            pltpu.VMEM((48, BLK, 128), F32),
            pltpu.VMEM((48, BLK, 128), BF),
            pltpu.VMEM((96, BLK, 128), F32),
        ],
        1_000_000_000,
        24,
    )(ids, parcels, same, other_low, other_high, hidden_grad)

    terms = lax.all_to_all(terms, "row", 0, 0, tiled=True)
    own = lax.optimization_barrier(lax.psum_scatter(part, COL, scatter_dimension=0, tiled=True))
    own = lax.dynamic_slice_in_dim(own, me_col, 384, 0)
    input_grad = call(input_end_kernel, shape(128, 384), 0, 1, [], 10_000_000, 4)(own)
    weight_grad = call(
        weight_end_kernel,
        shape(1, 4, 4096),
        2,
        1,
        [pltpu.VMEM((128, 128), F32)],
        500_000_000,
        4,
    )(panel_counts, first, terms)
    return hidden, input_grad, weight_grad


def solution(mesh):
    n_row, n_col = mesh.devices.shape
    fine = Mesh(mesh.devices.reshape(n_row, n_col // 2, 2), ("row", *COL))
    placed = (
        P("row", COL),
        P(COL, "row", None),
        P(COL, "row"),
        P(COL, "row"),
        P(COL),
        P("row", COL),
    )
    return jax.shard_map(
        on_device,
        mesh=fine,
        in_specs=placed,
        out_specs=(P("row", COL), P("row", COL), P(COL, "row", None)),
        check_vma=False,
    )
```

```python
import jax
import jax.numpy as jnp
from jax import lax
from jax.experimental import pallas as pl
from jax.experimental.pallas import tpu as pltpu
from jax.sharding import Mesh
from jax.sharding import PartitionSpec as P

root_two_pi = 0.7978845608028654
cubic_term = 0.044715
BF = jnp.bfloat16
F32 = jnp.float32
BLK = 64
NN = (((1,), (0,)), ((), ()))
NT = (((1,), (1,)), ((), ()))
TN = (((0,), (0,)), ((), ()))
COL = ("half", "side")
SM = pl.BlockSpec(memory_space=pltpu.SMEM)
VM = pl.BlockSpec(memory_space=pltpu.VMEM)
ANY = pl.BlockSpec(memory_space=pl.ANY)
MIB = 1 << 20


def dot(a, b, dims=NN):
    return lax.dot_general(a, b, dims, preferred_element_type=F32)


def picker(parted):
    i = lax.broadcasted_iota(jnp.int32, (128, 128), 0)
    j = lax.broadcasted_iota(jnp.int32, (128, 128), 1)
    place = i // 64 * 64 + i % 32 * 2 + i % 64 // 32
    return ((place if parted else i) == j).astype(BF)


def fetch(sems, *pairs):
    copies = [pltpu.make_async_copy(a, b, sems.at[i]) for i, (a, b) in enumerate(pairs)]
    for copy in copies:
        copy.start()
    return copies


def prep_kernel(
    first, rows_at, columns_at, count_at, blocks_at, tokens_at, parcels, turned, rows, columns, count, blocks, tokens, spread, sems
):
    for copy in fetch(
        sems, (blocks_at, blocks), (tokens_at, tokens), (rows_at, rows), (columns_at, columns), (count_at, count)
    ):
        copy.wait()
    for i in range(32):
        spread[pl.ds(i, 4, stride=32), :] = blocks[0, :, i * 128 : (i + 1) * 128].astype(F32)
    slot = first[0] + lax.broadcasted_iota(jnp.int32, (128, 128), 0) // 32
    parcels[0, :128] = jnp.where(slot < count[0], spread[...], 0.0).astype(BF)
    lane = lax.broadcasted_iota(jnp.int32, (16, 128), 1)
    named = jnp.zeros((16, 128), jnp.int32)
    for j in range(4):
        named = jnp.where(lane == j, rows[0, j], named)
        named = jnp.where(lane == 4 + j, columns[0, j], named)
    parcels[0, 128:] = named.astype(F32).astype(BF)

    def again(d, carry):
        parcels[d] = parcels[0]
        return carry

    lax.fori_loop(1, parcels.shape[0], again, 0)
    parted = picker(True)
    for k in range(3):
        at = k * 128
        turned[at : at + 128] = dot(parted, tokens[:, at : at + 128], NT).astype(BF)


def main_kernel(
    ids, weights_at, same, other_low, other_high, upstream_at, hidden, part, terms, weights, whole, upstream, pre, grad, total, sems
):
    copies = fetch(
        sems,
        (weights_at, weights),
        (same, whole.at[:48]),
        (other_low, whole.at[48:72]),
        (other_high, whole.at[72:]),
        (upstream_at, upstream),
    )
    pre[...] = jnp.zeros_like(pre)
    total[...] = jnp.zeros_like(total)
    for copy in copies[:4]:
        copy.wait()

    def slots(visit):
        def some(g, carry):
            for q in range(8):
                for j in range(4):
                    visit(g * 8 + q, j)
            return carry

        lax.fori_loop(0, 4, some, 0)

    def block(d, j):
        lines = weights[d, j * 32 : (j + 1) * 32]
        return jnp.concatenate([lines[:, :BLK], lines[:, BLK:]], axis=0)

    def forward(d, j):
        pre[ids[d, 4 + j]] += dot(block(d, j), whole[ids[d, j]], TN)

    slots(forward)
    copies[4].wait()
    unit = picker(False)

    def some_columns(g, carry):
        at = pl.multiple_of(g * 128, 128)
        v = pre[pl.ds(g * 2, 2)].reshape(128, 128)
        tangent = jnp.tanh(root_two_pi * (v + cubic_term * v * v * v))
        value = 0.5 * v * (1.0 + tangent)
        slope = 0.5 * (1.0 + tangent) + 0.5 * v * (1.0 - tangent * tangent) * root_two_pi * (
            1.0 + 3.0 * cubic_term * v * v
        )
        turned = dot(unit, upstream[:, pl.ds(at, 128)], NT)
        grad[pl.ds(g * 2, 2)] = (turned * slope).astype(BF).reshape(2, BLK, 128)
        hidden[:, pl.ds(at, 128)] = dot(unit, value.astype(BF), NT).astype(BF)
        return carry

    lax.fori_loop(0, 24, some_columns, 0, unroll=4)

    def weight(d, j):
        product = dot(whole[ids[d, j]], grad[ids[d, 4 + j]], NT).astype(BF)
        terms[d, j * 32 : (j + 1) * 32] = jnp.concatenate([product[:32], product[32:]], axis=1)

    slots(weight)

    def backward(d, j):
        total[ids[d, 8 + j]] += dot(block(d, j), grad[ids[d, 4 + j]])

    slots(backward)
    for o in range(16):
        part[400 * o : 400 * o + 384] = total[6 * o : 6 * o + 6].reshape(384, 128).astype(BF)
        if o < 15:
            part[400 * o + 384 : 400 * o + 400] = jnp.zeros((16, 128), BF)


def weight_end_kernel(count, first, terms, out, total):
    def some(d, kept):
        return kept + terms[d].astype(F32)

    kept = lax.fori_loop(1, terms.shape[0], some, terms[0].astype(F32))
    slot = first[0] + lax.broadcasted_iota(jnp.int32, (128, 128), 0) // 32
    total[...] = jnp.where(slot < count[0], kept, 0.0)
    for i in range(32):
        out[0, :, i * 128 : (i + 1) * 128] = total[pl.ds(i, 4, stride=32), :].astype(BF)


def input_end_kernel(own, out):
    parted = picker(True)
    for k in range(3):
        at = k * 128
        out[:, at : at + 128] = dot(own[at : at + 128], parted, TN).astype(BF)


def shape(*dims):
    return jax.ShapeDtypeStruct(dims, BF)


def call(kernel, outs, n_scalar, n_array, scratch, flops, limit, place=VM):
    return pl.pallas_call(
        kernel,
        out_shape=outs,
        in_specs=[SM] * n_scalar + [place] * n_array,
        out_specs=jax.tree.map(lambda _: VM, outs),
        scratch_shapes=scratch,
        compiler_params=pltpu.CompilerParams(vmem_limit_bytes=limit * MIB),
        cost_estimate=pl.CostEstimate(flops=flops, bytes_accessed=2 * MIB, transcendentals=0),
    )


def on_device(tokens, weight_blocks, block_rows, block_columns, panel_counts, hidden_grad):
    n_row, n_col = lax.axis_size("row"), lax.axis_size(COL)
    me_row, me_col, me_side = lax.axis_index("row"), lax.axis_index(COL), lax.axis_index("side")
    first = (me_row * 4).reshape(1)

    def shift(a, by):
        return lax.ppermute(a, COL, [(i, (i + by) % n_col) for i in range(n_col)])

    parcels, turned = call(
        prep_kernel,
        (shape(n_row, 144, 128), shape(384, 128)),
        1,
        5,
        [
            pltpu.SMEM((1, 4), jnp.int32),
            pltpu.SMEM((1, 4), jnp.int32),
            pltpu.SMEM((1,), jnp.int32),
            pltpu.VMEM((1, 4, 4096), BF),
            pltpu.VMEM((128, 384), BF),
            pltpu.VMEM((128, 128), F32),
            pltpu.SemaphoreType.DMA((5,)),
        ],
        10_000_000,
        60,
        ANY,
    )(first, block_rows, block_columns, panel_counts, weight_blocks, tokens)
    parcels = lax.all_to_all(parcels, "row", 0, 0, tiled=True)
    ids = parcels[:, 128, :8].astype(jnp.int32)
    owner = ids[:, :4] // 6
    rows = jnp.where(owner % 2 == me_side, 0, 48) + owner // 2 * 6 + ids[:, :4] % 6
    ids = jnp.concatenate([rows, ids[:, 4:], ids[:, :4]], axis=1)

    same = lax.all_gather(turned, "half", axis=0, tiled=True)
    middle = same.shape[0] // 2
    other_low, other_high = shift(same[:middle], 1), shift(same[middle:], -1)

    hidden, part, terms = call(
        main_kernel,
        (shape(128, 3072), shape(6384, 128), shape(n_row, 128, 128)),
        1,
        5,
        [
            pltpu.VMEM((n_row, 144, 128), BF),
            pltpu.VMEM((96, BLK, 128), BF),
            pltpu.VMEM((128, 3072), BF),
            pltpu.VMEM((48, BLK, 128), F32),
            pltpu.VMEM((48, BLK, 128), BF),
            pltpu.VMEM((96, BLK, 128), F32),
            pltpu.SemaphoreType.DMA((5,)),
        ],
        1_000_000_000,
        52,
        ANY,
    )(ids, parcels, *(a.reshape(-1, BLK, 128) for a in (same, other_low, other_high)), hidden_grad)

    terms = lax.all_to_all(terms, "row", 0, 0, tiled=True)
    own = lax.optimization_barrier(lax.psum_scatter(part, COL, scatter_dimension=0, tiled=True))
    own = lax.dynamic_slice_in_dim(own, me_col, 384, 0)
    input_grad = call(input_end_kernel, shape(128, 384), 0, 1, [], 10_000_000, 4)(own)
    weight_grad = call(
        weight_end_kernel,
        shape(1, 4, 4096),
        2,
        1,
        [pltpu.VMEM((128, 128), F32)],
        500_000_000,
        4,
    )(panel_counts, first, terms)
    return hidden, input_grad, weight_grad


def solution(mesh):
    n_row, n_col = mesh.devices.shape
    fine = Mesh(mesh.devices.reshape(n_row, n_col // 2, 2), ("row", *COL))
    placed = (
        P("row", COL),
        P(COL, "row", None),
        P(COL, "row"),
        P(COL, "row"),
        P(COL),
        P("row", COL),
    )
    return jax.shard_map(
        on_device,
        mesh=fine,
        in_specs=placed,
        out_specs=(P("row", COL), P("row", COL), P(COL, "row", None)),
        check_vma=False,
    )
```

```python
import jax
import jax.numpy as jnp
from jax import lax
from jax.experimental import pallas as pl
from jax.experimental.pallas import tpu as pltpu
from jax.sharding import Mesh
from jax.sharding import PartitionSpec as P

root_two_pi = 0.7978845608028654
cubic_term = 0.044715
BF = jnp.bfloat16
F32 = jnp.float32
BLK = 64
NN = (((1,), (0,)), ((), ()))
NT = (((1,), (1,)), ((), ()))
TN = (((0,), (0,)), ((), ()))
COL = ("half", "side")
SM = pl.BlockSpec(memory_space=pltpu.SMEM)
VM = pl.BlockSpec(memory_space=pltpu.VMEM)
ANY = pl.BlockSpec(memory_space=pl.ANY)
MIB = 1 << 20


def dot(a, b, dims=NN):
    return lax.dot_general(a, b, dims, preferred_element_type=F32)


def picker(parted):
    i = lax.broadcasted_iota(jnp.int32, (128, 128), 0)
    j = lax.broadcasted_iota(jnp.int32, (128, 128), 1)
    place = i // 64 * 64 + i % 32 * 2 + i % 64 // 32
    return ((place if parted else i) == j).astype(BF)


def fetch(sems, *pairs):
    copies = [pltpu.make_async_copy(a, b, sems.at[i]) for i, (a, b) in enumerate(pairs)]
    for copy in copies:
        copy.start()
    return copies


def prep_kernel(
    first, rows_at, columns_at, count_at, blocks_at, tokens_at, parcels, turned, rows, columns, count, blocks, tokens, spread, parcel, sems
):
    for copy in fetch(
        sems, (blocks_at, blocks), (tokens_at, tokens), (rows_at, rows), (columns_at, columns), (count_at, count)
    ):
        copy.wait()
    for i in range(32):
        spread[pl.ds(i, 4, stride=32), :] = blocks[0, :, i * 128 : (i + 1) * 128].astype(F32)
    slot = first[0] + lax.broadcasted_iota(jnp.int32, (128, 128), 0) // 32
    parcel[:128] = jnp.where(slot < count[0], spread[...], 0.0).astype(BF)
    lane = lax.broadcasted_iota(jnp.int32, (16, 128), 1)
    named = jnp.zeros((16, 128), jnp.int32)
    for j in range(4):
        named = jnp.where(lane == j, rows[0, j], named)
        named = jnp.where(lane == 4 + j, columns[0, j], named)
    parcel[128:] = named.astype(F32).astype(BF)
    copies = fetch(sems, *((parcel, parcels.at[d]) for d in range(parcels.shape[0])))
    parted = picker(True)
    for k in range(3):
        at = k * 128
        turned[at : at + 128] = dot(parted, tokens[:, at : at + 128], NT).astype(BF)
    for copy in copies:
        copy.wait()


def main_kernel(
    ids,
    weights_at,
    same,
    other_low,
    other_high,
    upstream_at,
    hidden_at,
    part_at,
    terms_at,
    weights,
    whole,
    upstream,
    hidden,
    part,
    terms,
    pre,
    grad,
    total,
    sems,
    out_sems,
):
    copies = fetch(
        sems,
        (weights_at, weights),
        (same, whole.at[:48]),
        (other_low, whole.at[48:72]),
        (other_high, whole.at[72:]),
        (upstream_at, upstream),
    )
    pre[...] = jnp.zeros_like(pre)
    total[...] = jnp.zeros_like(total)
    part[:, 384:] = jnp.zeros((16, 16, 128), BF)
    for copy in copies[:4]:
        copy.wait()

    def slots(visit, step):
        def some(g, carry):
            for q in range(step):
                for j in range(4):
                    visit(g * step + q, j)
            return carry

        lax.fori_loop(0, 32 // step, some, 0)

    def block(d, j):
        lines = weights[d, j * 32 : (j + 1) * 32]
        return jnp.concatenate([lines[:, :BLK], lines[:, BLK:]], axis=0)

    def forward(d, j):
        pre[ids[d, 4 + j]] += dot(block(d, j), whole[ids[d, j]], TN)

    slots(forward, 8)
    copies[4].wait()
    unit = picker(False)

    def some_columns(g, carry):
        at = pl.multiple_of(g * 128, 128)
        v = pre[pl.ds(g * 2, 2)].reshape(128, 128)
        tangent = jnp.tanh(root_two_pi * (v + cubic_term * v * v * v))
        value = 0.5 * v * (1.0 + tangent)
        slope = 0.5 * (1.0 + tangent) + 0.5 * v * (1.0 - tangent * tangent) * root_two_pi * (
            1.0 + 3.0 * cubic_term * v * v
        )
        turned = dot(unit, upstream[:, pl.ds(at, 128)], NT)
        grad[pl.ds(g * 2, 2)] = (turned * slope).astype(BF).reshape(2, BLK, 128)
        hidden[:, pl.ds(at, 128)] = dot(unit, value.astype(BF), NT).astype(BF)
        return carry

    lax.fori_loop(0, 24, some_columns, 0, unroll=4)
    sent = [pltpu.make_async_copy(hidden, hidden_at, out_sems.at[16])]
    sent[-1].start()

    def weight(d, j):
        product = dot(whole[ids[d, j]], grad[ids[d, 4 + j]], NT).astype(BF)
        terms[d, j * 32 : (j + 1) * 32] = jnp.concatenate([product[:32], product[32:]], axis=1)

    slots(weight, 16)
    sent.append(pltpu.make_async_copy(terms, terms_at, out_sems.at[17]))
    sent[-1].start()

    def backward(d, j):
        total[ids[d, 8 + j]] += dot(block(d, j), grad[ids[d, 4 + j]])

    slots(backward, 16)
    for o in range(16):
        part[o, :384] = total[6 * o : 6 * o + 6].reshape(384, 128).astype(BF)
        here, size = (part.at[o], 400) if o < 15 else (part.at[o, :384], 384)
        sent.append(pltpu.make_async_copy(here, part_at.at[400 * o : 400 * o + size], out_sems.at[o]))
        sent[-1].start()
    for copy in sent:
        copy.wait()


def end_kernel(count, first, terms, own, weights, inputs, total):
    def some(d, kept):
        return kept + terms[d].astype(F32)

    kept = lax.fori_loop(1, terms.shape[0], some, terms[0].astype(F32))
    slot = first[0] + lax.broadcasted_iota(jnp.int32, (128, 128), 0) // 32
    total[...] = jnp.where(slot < count[0], kept, 0.0)
    for i in range(32):
        weights[0, :, i * 128 : (i + 1) * 128] = total[pl.ds(i, 4, stride=32), :].astype(BF)
    parted = picker(True)
    for k in range(3):
        at = k * 128
        inputs[:, at : at + 128] = dot(own[at : at + 128], parted, TN).astype(BF)


def shape(*dims):
    return jax.ShapeDtypeStruct(dims, BF)


def call(kernel, outs, n_scalar, n_array, scratch, flops, limit, place, leave):
    return pl.pallas_call(
        kernel,
        out_shape=outs,
        in_specs=[SM] * n_scalar + [place] * n_array,
        out_specs=leave,
        scratch_shapes=scratch,
        compiler_params=pltpu.CompilerParams(vmem_limit_bytes=limit * MIB),
        cost_estimate=pl.CostEstimate(flops=flops, bytes_accessed=2 * MIB, transcendentals=0),
    )


def on_device(tokens, weight_blocks, block_rows, block_columns, panel_counts, hidden_grad):
    n_row, n_col = lax.axis_size("row"), lax.axis_size(COL)
    me_row, me_col, me_side = lax.axis_index("row"), lax.axis_index(COL), lax.axis_index("side")
    first = (me_row * 4).reshape(1)

    def shift(a, by):
        return lax.ppermute(a, COL, [(i, (i + by) % n_col) for i in range(n_col)])

    parcels, turned = call(
        prep_kernel,
        (shape(n_row, 144, 128), shape(384, 128)),
        1,
        5,
        [
            pltpu.SMEM((1, 4), jnp.int32),
            pltpu.SMEM((1, 4), jnp.int32),
            pltpu.SMEM((1,), jnp.int32),
            pltpu.VMEM((1, 4, 4096), BF),
            pltpu.VMEM((128, 384), BF),
            pltpu.VMEM((128, 128), F32),
            pltpu.VMEM((144, 128), BF),
            pltpu.SemaphoreType.DMA((n_row,)),
        ],
        10_000_000,
        60,
        ANY,
        (ANY, VM),
    )(first, block_rows, block_columns, panel_counts, weight_blocks, tokens)
    parcels = lax.all_to_all(parcels, "row", 0, 0, tiled=True)
    ids = parcels[:, 128, :8].astype(jnp.int32)
    owner = ids[:, :4] // 6
    rows = jnp.where(owner % 2 == me_side, 0, 48) + owner // 2 * 6 + ids[:, :4] % 6
    ids = jnp.concatenate([rows, ids[:, 4:], ids[:, :4]], axis=1)

    same = lax.all_gather(turned, "half", axis=0, tiled=True)
    middle = same.shape[0] // 2
    other_low, other_high = shift(same[:middle], 1), shift(same[middle:], -1)

    hidden, part, terms = call(
        main_kernel,
        (shape(128, 3072), shape(6384, 128), shape(n_row, 128, 128)),
        1,
        5,
        [
            pltpu.VMEM((n_row, 144, 128), BF),
            pltpu.VMEM((96, BLK, 128), BF),
            pltpu.VMEM((128, 3072), BF),
            pltpu.VMEM((128, 3072), BF),
            pltpu.VMEM((16, 400, 128), BF),
            pltpu.VMEM((n_row, 128, 128), BF),
            pltpu.VMEM((48, BLK, 128), F32),
            pltpu.VMEM((48, BLK, 128), BF),
            pltpu.VMEM((96, BLK, 128), F32),
            pltpu.SemaphoreType.DMA((5,)),
            pltpu.SemaphoreType.DMA((18,)),
        ],
        1_000_000_000,
        52,
        ANY,
        (ANY, ANY, ANY),
    )(ids, parcels, *(a.reshape(-1, BLK, 128) for a in (same, other_low, other_high)), hidden_grad)

    terms = lax.all_to_all(terms, "row", 0, 0, tiled=True)
    own = lax.optimization_barrier(lax.psum_scatter(part, COL, scatter_dimension=0, tiled=True))
    own = lax.dynamic_slice_in_dim(own, me_col, 384, 0)
    weight_grad, input_grad = call(
        end_kernel,
        (shape(1, 4, 4096), shape(128, 384)),
        2,
        2,
        [pltpu.VMEM((128, 128), F32)],
        10_000_000,
        4,
        VM,
        (VM, VM),
    )(panel_counts, first, terms, own)
    return hidden, input_grad, weight_grad


def solution(mesh):
    n_row, n_col = mesh.devices.shape
    fine = Mesh(mesh.devices.reshape(n_row, n_col // 2, 2), ("row", *COL))
    placed = (
        P("row", COL),
        P(COL, "row", None),
        P(COL, "row"),
        P(COL, "row"),
        P(COL),
        P("row", COL),
    )
    return jax.shard_map(
        on_device,
        mesh=fine,
        in_specs=placed,
        out_specs=(P("row", COL), P("row", COL), P(COL, "row", None)),
        check_vma=False,
    )
```

```python
import jax
import jax.numpy as jnp
from jax import lax
from jax.experimental import pallas as pl
from jax.experimental.pallas import tpu as pltpu
from jax.sharding import Mesh
from jax.sharding import PartitionSpec as P

root_two_pi = 0.7978845608028654
cubic_term = 0.044715
BF = jnp.bfloat16
F32 = jnp.float32
BLK = 64
NN = (((1,), (0,)), ((), ()))
NT = (((1,), (1,)), ((), ()))
TN = (((0,), (0,)), ((), ()))
COL = ("half", "side")
SM = pl.BlockSpec(memory_space=pltpu.SMEM)
VM = pl.BlockSpec(memory_space=pltpu.VMEM)
ANY = pl.BlockSpec(memory_space=pl.ANY)
MIB = 1 << 20


def dot(a, b, dims=NN):
    return lax.dot_general(a, b, dims, preferred_element_type=F32)


def picker(parted):
    i = lax.broadcasted_iota(jnp.int32, (128, 128), 0)
    j = lax.broadcasted_iota(jnp.int32, (128, 128), 1)
    place = i // 64 * 64 + i % 32 * 2 + i % 64 // 32
    return ((place if parted else i) == j).astype(BF)


def fetch(sems, *pairs):
    copies = [pltpu.make_async_copy(a, b, sems.at[i]) for i, (a, b) in enumerate(pairs)]
    for copy in copies:
        copy.start()
    return copies


def prep_kernel(
    first, rows_at, columns_at, count_at, blocks_at, tokens_at, parcels, turned, rows, columns, count, blocks, tokens, spread, sems
):
    for copy in fetch(
        sems, (blocks_at, blocks), (tokens_at, tokens), (rows_at, rows), (columns_at, columns), (count_at, count)
    ):
        copy.wait()
    for i in range(32):
        spread[pl.ds(i, 4, stride=32), :] = blocks[0, :, i * 128 : (i + 1) * 128].astype(F32)
    slot = first[0] + lax.broadcasted_iota(jnp.int32, (128, 128), 0) // 32
    parcels[0, :128] = jnp.where(slot < count[0], spread[...], 0.0).astype(BF)
    lane = lax.broadcasted_iota(jnp.int32, (16, 128), 1)
    named = jnp.zeros((16, 128), jnp.int32)
    for j in range(4):
        named = jnp.where(lane == j, rows[0, j], named)
        named = jnp.where(lane == 4 + j, columns[0, j], named)
    parcels[0, 128:] = named.astype(F32).astype(BF)

    def again(d, carry):
        parcels[d] = parcels[0]
        return carry

    lax.fori_loop(1, parcels.shape[0], again, 0)
    parted = picker(True)
    for k in range(3):
        at = k * 128
        turned[at : at + 128] = dot(parted, tokens[:, at : at + 128], NT).astype(BF)


def forward(entry, weights, whole, pre):
    slot = jnp.bitwise_and(entry, 127)
    column = jnp.bitwise_and(jnp.right_shift(entry, 7), 63)
    row = jnp.right_shift(entry, 13)
    start = pl.multiple_of(jnp.bitwise_and(slot, 3) * 32, 32)
    lines = weights[jnp.right_shift(slot, 2), pl.ds(start, 32)]
    block = jnp.concatenate([lines[:, :BLK], lines[:, BLK:]], axis=0)
    pre[column] += dot(block, whole[row], TN)


def forward_all(count, at, entries, weights, whole, pre):
    def some(g, carry):
        for i in range(16):
            forward(entries[at + g * 16 + i], weights, whole, pre)
        return carry

    lax.fori_loop(0, jnp.right_shift(count + 15, 4), some, 0)


def early_kernel(
    ids,
    weights_at,
    same,
    upstream_at,
    early_at,
    turned_at,
    later,
    weights,
    whole,
    upstream,
    pre,
    turned,
    now,
    sems,
    out_sems,
):
    copies = fetch(sems, (upstream_at, upstream), (weights_at, weights), (same, whole))
    pre[...] = jnp.zeros_like(pre)

    def sort(d, counts):
        n, m = counts
        for j in range(4):
            row = ids[d, j]
            entry = (row * 64 + ids[d, 4 + j]) * 128 + d * 4 + j
            far = (row >= 48).astype(jnp.int32)
            now[n] = entry
            later[1 + m] = entry
            n, m = n + 1 - far, m + far
        return n, m

    n, m = lax.fori_loop(0, 32, sort, (jnp.int32(0), jnp.int32(0)))
    for i in range(16):
        now[n + i] = 48 * 128
        later[1 + m + i] = (48 * 64 + 48) * 128
    later[0] = m
    unit = picker(False)
    copies[0].wait()

    def some_columns(g, carry):
        at = pl.multiple_of(g * 128, 128)
        turned[pl.ds(g * 2, 2)] = dot(unit, upstream[:, pl.ds(at, 128)], NT).astype(BF).reshape(2, BLK, 128)
        return carry

    lax.fori_loop(0, 24, some_columns, 0, unroll=4)
    sent = fetch(out_sems.at[:1], (turned, turned_at))
    for copy in copies[1:]:
        copy.wait()
    forward_all(n, 0, now, weights, whole, pre)
    sent += fetch(out_sems.at[1:], (pre.at[:48], early_at))
    for copy in sent:
        copy.wait()


def main_kernel(
    ids,
    entries,
    weights_at,
    same,
    other_low,
    other_high,
    early_at,
    turned_at,
    hidden_at,
    part_at,
    terms_at,
    weights,
    whole,
    early,
    turned,
    hidden,
    part,
    terms,
    pre,
    grad,
    total,
    sems,
    out_sems,
):
    copies = fetch(
        sems,
        (weights_at, weights),
        (other_low, whole.at[48:72]),
        (other_high, whole.at[72:]),
        (early_at, early),
        (turned_at, turned),
        (same, whole.at[:48]),
    )
    pre[...] = jnp.zeros_like(pre)
    total[...] = jnp.zeros_like(total)
    part[:, 384:] = jnp.zeros((16, 16, 128), BF)
    for copy in copies[:3]:
        copy.wait()

    def slots(visit, step):
        def some(g, carry):
            for q in range(step):
                for j in range(4):
                    visit(g * step + q, j)
            return carry

        lax.fori_loop(0, 32 // step, some, 0)

    def block(d, j):
        lines = weights[d, j * 32 : (j + 1) * 32]
        return jnp.concatenate([lines[:, :BLK], lines[:, BLK:]], axis=0)

    forward_all(entries[0], 1, entries, weights, whole, pre)
    for copy in copies[3:]:
        copy.wait()
    unit = picker(False)

    def some_columns(g, carry):
        at = pl.multiple_of(g * 128, 128)
        v = (pre[pl.ds(g * 2, 2)] + early[pl.ds(g * 2, 2)]).reshape(128, 128)
        tangent = jnp.tanh(root_two_pi * (v + cubic_term * v * v * v))
        value = 0.5 * v * (1.0 + tangent)
        slope = 0.5 * (1.0 + tangent) + 0.5 * v * (1.0 - tangent * tangent) * root_two_pi * (
            1.0 + 3.0 * cubic_term * v * v
        )
        upstream = turned[pl.ds(g * 2, 2)].reshape(128, 128).astype(F32)
        grad[pl.ds(g * 2, 2)] = (upstream * slope).astype(BF).reshape(2, BLK, 128)
        hidden[:, pl.ds(at, 128)] = dot(unit, value.astype(BF), NT).astype(BF)
        return carry

    lax.fori_loop(0, 24, some_columns, 0, unroll=4)
    sent = [pltpu.make_async_copy(hidden, hidden_at, out_sems.at[16])]
    sent[-1].start()

    def weight(d, j):
        product = dot(whole[ids[d, j]], grad[ids[d, 4 + j]], NT).astype(BF)
        terms[d, j * 32 : (j + 1) * 32] = jnp.concatenate([product[:32], product[32:]], axis=1)

    slots(weight, 16)
    sent.append(pltpu.make_async_copy(terms, terms_at, out_sems.at[17]))
    sent[-1].start()

    def backward(d, j):
        total[ids[d, 8 + j]] += dot(block(d, j), grad[ids[d, 4 + j]])

    slots(backward, 16)
    for o in range(16):
        part[o, :384] = total[6 * o : 6 * o + 6].reshape(384, 128).astype(BF)
        here, size = (part.at[o], 400) if o < 15 else (part.at[o, :384], 384)
        sent.append(pltpu.make_async_copy(here, part_at.at[400 * o : 400 * o + size], out_sems.at[o]))
        sent[-1].start()
    for copy in sent:
        copy.wait()


def end_kernel(count, first, terms, own, weights, inputs, total):
    def some(d, kept):
        return kept + terms[d].astype(F32)

    kept = lax.fori_loop(1, terms.shape[0], some, terms[0].astype(F32))
    slot = first[0] + lax.broadcasted_iota(jnp.int32, (128, 128), 0) // 32
    total[...] = jnp.where(slot < count[0], kept, 0.0)
    for i in range(32):
        weights[0, :, i * 128 : (i + 1) * 128] = total[pl.ds(i, 4, stride=32), :].astype(BF)
    parted = picker(True)
    for k in range(3):
        at = k * 128
        inputs[:, at : at + 128] = dot(own[at : at + 128], parted, TN).astype(BF)


def shape(*dims):
    return jax.ShapeDtypeStruct(dims, BF)


def call(kernel, outs, n_scalar, n_array, scratch, flops, limit, place, leave):
    return pl.pallas_call(
        kernel,
        out_shape=outs,
        in_specs=[SM] * n_scalar + [place] * n_array,
        out_specs=leave,
        scratch_shapes=scratch,
        compiler_params=pltpu.CompilerParams(vmem_limit_bytes=limit * MIB),
        cost_estimate=pl.CostEstimate(flops=flops, bytes_accessed=2 * MIB, transcendentals=0),
    )


def on_device(tokens, weight_blocks, block_rows, block_columns, panel_counts, hidden_grad):
    n_row, n_col = lax.axis_size("row"), lax.axis_size(COL)
    me_row, me_col, me_side = lax.axis_index("row"), lax.axis_index(COL), lax.axis_index("side")
    first = (me_row * 4).reshape(1)

    def shift(a, by):
        return lax.ppermute(a, COL, [(i, (i + by) % n_col) for i in range(n_col)])

    parcels, turned = call(
        prep_kernel,
        (shape(n_row, 144, 128), shape(384, 128)),
        1,
        5,
        [
            pltpu.SMEM((1, 4), jnp.int32),
            pltpu.SMEM((1, 4), jnp.int32),
            pltpu.SMEM((1,), jnp.int32),
            pltpu.VMEM((1, 4, 4096), BF),
            pltpu.VMEM((128, 384), BF),
            pltpu.VMEM((128, 128), F32),
            pltpu.SemaphoreType.DMA((5,)),
        ],
        10_000_000,
        60,
        ANY,
        (VM, VM),
    )(first, block_rows, block_columns, panel_counts, weight_blocks, tokens)
    parcels = lax.all_to_all(parcels, "row", 0, 0, tiled=True)
    ids = parcels[:, 128, :8].astype(jnp.int32)
    owner = ids[:, :4] // 6
    rows = jnp.where(owner % 2 == me_side, 0, 48) + owner // 2 * 6 + ids[:, :4] % 6
    ids = jnp.concatenate([rows, ids[:, 4:], ids[:, :4]], axis=1)

    same = lax.all_gather(turned, "half", axis=0, tiled=True)
    middle = same.shape[0] // 2
    other_low, other_high = shift(same[:middle], 1), shift(same[middle:], -1)

    same, other_low, other_high = (a.reshape(-1, BLK, 128) for a in (same, other_low, other_high))
    early, turned, entries = call(
        early_kernel,
        (
            jax.ShapeDtypeStruct((48, BLK, 128), F32),
            shape(48, BLK, 128),
            jax.ShapeDtypeStruct((160,), jnp.int32),
        ),
        1,
        3,
        [
            pltpu.VMEM((n_row, 144, 128), BF),
            pltpu.VMEM((48, BLK, 128), BF),
            pltpu.VMEM((128, 3072), BF),
            pltpu.VMEM((49, BLK, 128), F32),
            pltpu.VMEM((48, BLK, 128), BF),
            pltpu.SMEM((160,), jnp.int32),
            pltpu.SemaphoreType.DMA((3,)),
            pltpu.SemaphoreType.DMA((2,)),
        ],
        500_000_000,
        52,
        ANY,
        (ANY, ANY, SM),
    )(ids, parcels, same, hidden_grad)

    hidden, part, terms = call(
        main_kernel,
        (shape(128, 3072), shape(6384, 128), shape(n_row, 128, 128)),
        2,
        6,
        [
            pltpu.VMEM((n_row, 144, 128), BF),
            pltpu.VMEM((96, BLK, 128), BF),
            pltpu.VMEM((48, BLK, 128), F32),
            pltpu.VMEM((48, BLK, 128), BF),
            pltpu.VMEM((128, 3072), BF),
            pltpu.VMEM((16, 400, 128), BF),
            pltpu.VMEM((n_row, 128, 128), BF),
            pltpu.VMEM((49, BLK, 128), F32),
            pltpu.VMEM((48, BLK, 128), BF),
            pltpu.VMEM((96, BLK, 128), F32),
            pltpu.SemaphoreType.DMA((6,)),
            pltpu.SemaphoreType.DMA((18,)),
        ],
        1_000_000_000,
        52,
        ANY,
        (ANY, ANY, ANY),
    )(ids, entries, parcels, same, other_low, other_high, early, turned)

    terms = lax.all_to_all(terms, "row", 0, 0, tiled=True)
    own = lax.optimization_barrier(lax.psum_scatter(part, COL, scatter_dimension=0, tiled=True))
    own = lax.dynamic_slice_in_dim(own, me_col, 384, 0)
    weight_grad, input_grad = call(
        end_kernel,
        (shape(1, 4, 4096), shape(128, 384)),
        2,
        2,
        [pltpu.VMEM((128, 128), F32)],
        10_000_000,
        4,
        VM,
        (VM, VM),
    )(panel_counts, first, terms, own)
    return hidden, input_grad, weight_grad


def solution(mesh):
    n_row, n_col = mesh.devices.shape
    fine = Mesh(mesh.devices.reshape(n_row, n_col // 2, 2), ("row", *COL))
    placed = (
        P("row", COL),
        P(COL, "row", None),
        P(COL, "row"),
        P(COL, "row"),
        P(COL),
        P("row", COL),
    )
    return jax.shard_map(
        on_device,
        mesh=fine,
        in_specs=placed,
        out_specs=(P("row", COL), P("row", COL), P(COL, "row", None)),
        check_vma=False,
    )
```

```python
import jax
import jax.numpy as jnp
from jax import lax
from jax.experimental import pallas as pl
from jax.experimental.pallas import tpu as pltpu
from jax.sharding import Mesh
from jax.sharding import PartitionSpec as P

root_two_pi = 0.7978845608028654
cubic_term = 0.044715
BF = jnp.bfloat16
F32 = jnp.float32
BLK = 64
NN = (((1,), (0,)), ((), ()))
NT = (((1,), (1,)), ((), ()))
TN = (((0,), (0,)), ((), ()))
COL = ("half", "side")
SM = pl.BlockSpec(memory_space=pltpu.SMEM)
VM = pl.BlockSpec(memory_space=pltpu.VMEM)
ANY = pl.BlockSpec(memory_space=pl.ANY)
MIB = 1 << 20


def dot(a, b, dims=NN):
    return lax.dot_general(a, b, dims, preferred_element_type=F32)


def picker(parted):
    i = lax.broadcasted_iota(jnp.int32, (128, 128), 0)
    j = lax.broadcasted_iota(jnp.int32, (128, 128), 1)
    place = i // 64 * 64 + i % 32 * 2 + i % 64 // 32
    return ((place if parted else i) == j).astype(BF)


def fetch(sems, *pairs):
    copies = [pltpu.make_async_copy(a, b, sems.at[i]) for i, (a, b) in enumerate(pairs)]
    for copy in copies:
        copy.start()
    return copies


def prep_kernel(
    first, rows_at, columns_at, count_at, blocks_at, tokens_at, parcels, turned, rows, columns, count, blocks, tokens, spread, sems
):
    for copy in fetch(
        sems, (blocks_at, blocks), (tokens_at, tokens), (rows_at, rows), (columns_at, columns), (count_at, count)
    ):
        copy.wait()
    for i in range(32):
        spread[pl.ds(i, 4, stride=32), :] = blocks[0, :, i * 128 : (i + 1) * 128].astype(F32)
    slot = first[0] + lax.broadcasted_iota(jnp.int32, (128, 128), 0) // 32
    parcels[0, :128] = jnp.where(slot < count[0], spread[...], 0.0).astype(BF)
    lane = lax.broadcasted_iota(jnp.int32, (16, 128), 1)
    named = jnp.zeros((16, 128), jnp.int32)
    for j in range(4):
        named = jnp.where(lane == j, rows[0, j], named)
        named = jnp.where(lane == 4 + j, columns[0, j], named)
    parcels[0, 128:] = named.astype(F32).astype(BF)

    def again(d, carry):
        parcels[d] = parcels[0]
        return carry

    lax.fori_loop(1, parcels.shape[0], again, 0)
    parted = picker(True)
    for k in range(3):
        at = k * 128
        turned[at : at + 128] = dot(parted, tokens[:, at : at + 128], NT).astype(BF)


def forward(entry, weights, whole, pre):
    slot = jnp.bitwise_and(entry, 127)
    column = jnp.bitwise_and(jnp.right_shift(entry, 7), 63)
    row = jnp.right_shift(entry, 13)
    start = pl.multiple_of(jnp.bitwise_and(slot, 3) * 32, 32)
    lines = weights[jnp.right_shift(slot, 2), pl.ds(start, 32)]
    block = jnp.concatenate([lines[:, :BLK], lines[:, BLK:]], axis=0)
    pre[column] += dot(block, whole[row], TN)


def forward_all(count, at, entries, weights, whole, pre):
    def some(g, carry):
        for i in range(16):
            forward(entries[at + g * 16 + i], weights, whole, pre)
        return carry

    lax.fori_loop(0, jnp.right_shift(count + 15, 4), some, 0)


def early_kernel(
    ids,
    weights_at,
    same,
    upstream_at,
    early_at,
    turned_at,
    later,
    weights,
    whole,
    upstream,
    pre,
    turned,
    now,
    sems,
    out_sems,
):
    copies = fetch(sems, (upstream_at, upstream), (weights_at, weights), (same, whole))
    pre[...] = jnp.zeros_like(pre)

    def sort(d, counts):
        n, m = counts
        for j in range(4):
            row = ids[d, j]
            entry = (row * 64 + ids[d, 4 + j]) * 128 + d * 4 + j
            far = (row >= 48).astype(jnp.int32)
            now[n] = entry
            later[1 + m] = entry
            n, m = n + 1 - far, m + far
        return n, m

    n, m = lax.fori_loop(0, 32, sort, (jnp.int32(0), jnp.int32(0)))
    for i in range(16):
        now[n + i] = 48 * 128
        later[1 + m + i] = (48 * 64 + 48) * 128
    later[0] = m
    unit = picker(False)
    copies[0].wait()

    def some_columns(g, carry):
        at = pl.multiple_of(g * 128, 128)
        turned[pl.ds(g * 2, 2)] = dot(unit, upstream[:, pl.ds(at, 128)], NT).astype(BF).reshape(2, BLK, 128)
        return carry

    lax.fori_loop(0, 24, some_columns, 0, unroll=4)
    sent = fetch(out_sems.at[:1], (turned, turned_at))
    for copy in copies[1:]:
        copy.wait()
    forward_all(n, 0, now, weights, whole, pre)
    sent += fetch(out_sems.at[1:], (pre.at[:48], early_at))
    for copy in sent:
        copy.wait()


def main_kernel(
    ids,
    entries,
    weights_at,
    same,
    other_low,
    other_high,
    early_at,
    turned_at,
    hidden_at,
    part_at,
    terms_at,
    weights,
    whole,
    early,
    turned,
    hidden,
    part,
    terms,
    pre,
    grad,
    total,
    sems,
    out_sems,
):
    copies = fetch(
        sems,
        (weights_at, weights),
        (other_low, whole.at[48:72]),
        (other_high, whole.at[72:]),
        (early_at, early),
        (turned_at, turned),
        (same, whole.at[:48]),
    )
    pre[...] = jnp.zeros_like(pre)
    total[...] = jnp.zeros_like(total)
    part[:, 384:] = jnp.zeros((16, 16, 128), BF)
    for copy in copies[:3]:
        copy.wait()

    def slots(visit, step):
        def some(g, carry):
            for q in range(step):
                for j in range(4):
                    visit(g * step + q, j)
            return carry

        lax.fori_loop(0, 32 // step, some, 0)

    def block(d, j):
        lines = weights[d, j * 32 : (j + 1) * 32]
        return jnp.concatenate([lines[:, :BLK], lines[:, BLK:]], axis=0)

    forward_all(entries[0], 1, entries, weights, whole, pre)
    for copy in copies[3:]:
        copy.wait()
    unit = picker(False)

    def some_columns(g, carry):
        at = pl.multiple_of(g * 128, 128)
        v = (pre[pl.ds(g * 2, 2)] + early[pl.ds(g * 2, 2)]).reshape(128, 128)
        tangent = jnp.tanh(root_two_pi * (v + cubic_term * v * v * v))
        value = 0.5 * v * (1.0 + tangent)
        slope = 0.5 * (1.0 + tangent) + 0.5 * v * (1.0 - tangent * tangent) * root_two_pi * (
            1.0 + 3.0 * cubic_term * v * v
        )
        upstream = turned[pl.ds(g * 2, 2)].reshape(128, 128).astype(F32)
        grad[pl.ds(g * 2, 2)] = (upstream * slope).astype(BF).reshape(2, BLK, 128)
        hidden[:, pl.ds(at, 128)] = dot(unit, value.astype(BF), NT).astype(BF)
        return carry

    lax.fori_loop(0, 24, some_columns, 0, unroll=4)
    sent = [pltpu.make_async_copy(hidden, hidden_at, out_sems.at[16])]
    sent[-1].start()

    def weight(d, j):
        product = dot(whole[ids[d, j]], grad[ids[d, 4 + j]], NT).astype(BF)
        terms[d, j * 32 : (j + 1) * 32] = jnp.concatenate([product[:32], product[32:]], axis=1)

    slots(weight, 16)
    sent.append(pltpu.make_async_copy(terms, terms_at, out_sems.at[17]))
    sent[-1].start()

    def backward(d, j):
        total[ids[d, 8 + j]] += dot(block(d, j), grad[ids[d, 4 + j]])

    slots(backward, 16)
    for o in range(16):
        part[o, :384] = total[6 * o : 6 * o + 6].reshape(384, 128).astype(BF)
        here, size = (part.at[o], 400) if o < 15 else (part.at[o, :384], 384)
        sent.append(pltpu.make_async_copy(here, part_at.at[400 * o : 400 * o + size], out_sems.at[o]))
        sent[-1].start()
    for copy in sent:
        copy.wait()


def end_kernel(count, first, terms, own, weights, inputs, total):
    def some(d, kept):
        return kept + terms[d].astype(F32)

    kept = lax.fori_loop(1, terms.shape[0], some, terms[0].astype(F32))
    slot = first[0] + lax.broadcasted_iota(jnp.int32, (128, 128), 0) // 32
    total[...] = jnp.where(slot < count[0], kept, 0.0)
    for i in range(32):
        weights[0, :, i * 128 : (i + 1) * 128] = total[pl.ds(i, 4, stride=32), :].astype(BF)
    parted = picker(True)
    for k in range(3):
        at = k * 128
        inputs[:, at : at + 128] = dot(own[at : at + 128], parted, TN).astype(BF)


def shape(*dims):
    return jax.ShapeDtypeStruct(dims, BF)


def call(kernel, outs, n_scalar, n_array, scratch, flops, limit, place, leave):
    return pl.pallas_call(
        kernel,
        out_shape=outs,
        in_specs=[SM] * n_scalar + [place] * n_array,
        out_specs=leave,
        scratch_shapes=scratch,
        compiler_params=pltpu.CompilerParams(vmem_limit_bytes=limit * MIB),
        cost_estimate=pl.CostEstimate(flops=flops, bytes_accessed=2 * MIB, transcendentals=0),
    )


def on_device(tokens, weight_blocks, block_rows, block_columns, panel_counts, hidden_grad):
    n_row, n_col = lax.axis_size("row"), lax.axis_size(COL)
    me_row, me_col, me_side = lax.axis_index("row"), lax.axis_index(COL), lax.axis_index("side")
    first = (me_row * 4).reshape(1)

    def shift(a, by):
        return lax.ppermute(a, COL, [(i, (i + by) % n_col) for i in range(n_col)])

    parcels, turned = call(
        prep_kernel,
        (shape(n_row, 144, 128), shape(384, 128)),
        1,
        5,
        [
            pltpu.SMEM((1, 4), jnp.int32),
            pltpu.SMEM((1, 4), jnp.int32),
            pltpu.SMEM((1,), jnp.int32),
            pltpu.VMEM((1, 4, 4096), BF),
            pltpu.VMEM((128, 384), BF),
            pltpu.VMEM((128, 128), F32),
            pltpu.SemaphoreType.DMA((5,)),
        ],
        10_000_000,
        60,
        ANY,
        (VM, VM),
    )(first, block_rows, block_columns, panel_counts, weight_blocks, tokens)
    parcels = lax.all_to_all(parcels, "row", 0, 0, tiled=True)
    ids = parcels[:, 128, :8].astype(jnp.int32)
    owner = ids[:, :4] // 6
    rows = jnp.where(owner % 2 == me_side, 0, 48) + owner // 2 * 6 + ids[:, :4] % 6
    ids = jnp.concatenate([rows, ids[:, 4:], ids[:, :4]], axis=1)

    same = lax.all_gather(turned, "half", axis=0, tiled=True)
    middle = same.shape[0] // 2
    other_low, other_high = shift(same[:middle], 1), shift(same[middle:], -1)

    same, other_low, other_high = (a.reshape(-1, BLK, 128) for a in (same, other_low, other_high))
    early, turned, entries = call(
        early_kernel,
        (
            jax.ShapeDtypeStruct((48, BLK, 128), F32),
            shape(48, BLK, 128),
            jax.ShapeDtypeStruct((160,), jnp.int32),
        ),
        1,
        3,
        [
            pltpu.VMEM((n_row, 144, 128), BF),
            pltpu.VMEM((48, BLK, 128), BF),
            pltpu.VMEM((128, 3072), BF),
            pltpu.VMEM((49, BLK, 128), F32),
            pltpu.VMEM((48, BLK, 128), BF),
            pltpu.SMEM((160,), jnp.int32),
            pltpu.SemaphoreType.DMA((3,)),
            pltpu.SemaphoreType.DMA((2,)),
        ],
        500_000_000,
        8,
        ANY,
        (ANY, ANY, SM),
    )(ids, parcels, same, hidden_grad)

    hidden, part, terms = call(
        main_kernel,
        (shape(128, 3072), shape(6384, 128), shape(n_row, 128, 128)),
        2,
        6,
        [
            pltpu.VMEM((n_row, 144, 128), BF),
            pltpu.VMEM((96, BLK, 128), BF),
            pltpu.VMEM((48, BLK, 128), F32),
            pltpu.VMEM((48, BLK, 128), BF),
            pltpu.VMEM((128, 3072), BF),
            pltpu.VMEM((16, 400, 128), BF),
            pltpu.VMEM((n_row, 128, 128), BF),
            pltpu.VMEM((49, BLK, 128), F32),
            pltpu.VMEM((48, BLK, 128), BF),
            pltpu.VMEM((96, BLK, 128), F32),
            pltpu.SemaphoreType.DMA((6,)),
            pltpu.SemaphoreType.DMA((18,)),
        ],
        1_000_000_000,
        48,
        ANY,
        (ANY, ANY, ANY),
    )(ids, entries, parcels, same, other_low, other_high, early, turned)

    terms = lax.all_to_all(terms, "row", 0, 0, tiled=True)
    own = lax.optimization_barrier(lax.psum_scatter(part, COL, scatter_dimension=0, tiled=True))
    own = lax.dynamic_slice_in_dim(own, me_col, 384, 0)
    weight_grad, input_grad = call(
        end_kernel,
        (shape(1, 4, 4096), shape(128, 384)),
        2,
        2,
        [pltpu.VMEM((128, 128), F32)],
        10_000_000,
        4,
        VM,
        (VM, VM),
    )(panel_counts, first, terms, own)
    return hidden, input_grad, weight_grad


def solution(mesh):
    n_row, n_col = mesh.devices.shape
    fine = Mesh(mesh.devices.reshape(n_row, n_col // 2, 2), ("row", *COL))
    placed = (
        P("row", COL),
        P(COL, "row", None),
        P(COL, "row"),
        P(COL, "row"),
        P(COL),
        P("row", COL),
    )
    return jax.shard_map(
        on_device,
        mesh=fine,
        in_specs=placed,
        out_specs=(P("row", COL), P("row", COL), P(COL, "row", None)),
        check_vma=False,
    )
```

```python
import jax
import jax.numpy as jnp
from jax import lax
from jax.experimental import pallas as pl
from jax.experimental.pallas import tpu as pltpu
from jax.sharding import Mesh
from jax.sharding import PartitionSpec as P

root_two_pi = 0.7978845608028654
cubic_term = 0.044715
BF = jnp.bfloat16
F32 = jnp.float32
BLK = 64
NN = (((1,), (0,)), ((), ()))
NT = (((1,), (1,)), ((), ()))
TN = (((0,), (0,)), ((), ()))
COL = ("half", "side")
SM = pl.BlockSpec(memory_space=pltpu.SMEM)
VM = pl.BlockSpec(memory_space=pltpu.VMEM)
ANY = pl.BlockSpec(memory_space=pl.ANY)
MIB = 1 << 20


def dot(a, b, dims=NN):
    return lax.dot_general(a, b, dims, preferred_element_type=F32)


def picker(parted):
    i = lax.broadcasted_iota(jnp.int32, (128, 128), 0)
    j = lax.broadcasted_iota(jnp.int32, (128, 128), 1)
    place = i // 64 * 64 + i % 32 * 2 + i % 64 // 32
    return ((place if parted else i) == j).astype(BF)


def fetch(sems, *pairs):
    copies = [pltpu.make_async_copy(a, b, sems.at[i]) for i, (a, b) in enumerate(pairs)]
    for copy in copies:
        copy.start()
    return copies


def prep_kernel(
    first, rows_at, columns_at, count_at, blocks_at, tokens_at, parcels, turned, rows, columns, count, blocks, tokens, spread, sems
):
    for copy in fetch(
        sems, (blocks_at, blocks), (tokens_at, tokens), (rows_at, rows), (columns_at, columns), (count_at, count)
    ):
        copy.wait()
    for i in range(32):
        spread[pl.ds(i, 4, stride=32), :] = blocks[0, :, i * 128 : (i + 1) * 128].astype(F32)
    slot = first[0] + lax.broadcasted_iota(jnp.int32, (128, 128), 0) // 32
    parcels[0, :128] = jnp.where(slot < count[0], spread[...], 0.0).astype(BF)
    lane = lax.broadcasted_iota(jnp.int32, (16, 128), 1)
    named = jnp.zeros((16, 128), jnp.int32)
    for j in range(4):
        named = jnp.where(lane == j, rows[0, j], named)
        named = jnp.where(lane == 4 + j, columns[0, j], named)
    parcels[0, 128:] = named.astype(F32).astype(BF)

    def again(d, carry):
        parcels[d] = parcels[0]
        return carry

    lax.fori_loop(1, parcels.shape[0], again, 0)
    parted = picker(True)
    for k in range(3):
        at = k * 128
        turned[at : at + 128] = dot(parted, tokens[:, at : at + 128], NT).astype(BF)


def forward(entry, weights, whole, pre):
    slot = jnp.bitwise_and(entry, 127)
    column = jnp.bitwise_and(jnp.right_shift(entry, 7), 63)
    row = jnp.right_shift(entry, 13)
    start = pl.multiple_of(jnp.bitwise_and(slot, 3) * 32, 32)
    lines = weights[jnp.right_shift(slot, 2), pl.ds(start, 32)]
    block = jnp.concatenate([lines[:, :BLK], lines[:, BLK:]], axis=0)
    pre[column] += dot(block, whole[row], TN)


def forward_all(count, at, entries, weights, whole, pre):
    def some(g, carry):
        for i in range(16):
            forward(entries[at + g * 16 + i], weights, whole, pre)
        return carry

    lax.fori_loop(0, jnp.right_shift(count + 15, 4), some, 0)


def early_kernel(
    ids,
    weights_at,
    same,
    upstream_at,
    early_at,
    turned_at,
    later,
    weights,
    whole,
    upstream,
    pre,
    turned,
    now,
    sems,
    out_sems,
):
    copies = fetch(sems, (upstream_at, upstream), (weights_at, weights), (same, whole))
    pre[...] = jnp.zeros_like(pre)

    def sort(d, counts):
        n, m = counts
        for j in range(4):
            row = ids[d, j]
            entry = (row * 64 + ids[d, 4 + j]) * 128 + d * 4 + j
            far = (row >= 48).astype(jnp.int32)
            now[n] = entry
            later[1 + m] = entry
            n, m = n + 1 - far, m + far
        return n, m

    n, m = lax.fori_loop(0, 32, sort, (jnp.int32(0), jnp.int32(0)))
    for i in range(16):
        now[n + i] = 48 * 128
        later[1 + m + i] = (48 * 64 + 48) * 128
    later[0] = m
    unit = picker(False)
    copies[0].wait()

    def some_columns(g, carry):
        at = pl.multiple_of(g * 128, 128)
        turned[pl.ds(g * 2, 2)] = dot(unit, upstream[:, pl.ds(at, 128)], NT).astype(BF).reshape(2, BLK, 128)
        return carry

    lax.fori_loop(0, 24, some_columns, 0, unroll=4)
    sent = fetch(out_sems.at[:1], (turned, turned_at))
    for copy in copies[1:]:
        copy.wait()
    forward_all(n, 0, now, weights, whole, pre)
    sent += fetch(out_sems.at[1:], (pre.at[:48], early_at))
    for copy in sent:
        copy.wait()


def main_kernel(
    ids,
    entries,
    weights_at,
    same,
    other_low,
    other_high,
    early_at,
    turned_at,
    hidden_at,
    part_at,
    terms_at,
    weights,
    whole,
    early,
    turned,
    hidden,
    part,
    terms,
    pre,
    grad,
    total,
    sems,
    out_sems,
):
    copies = fetch(
        sems,
        (weights_at, weights),
        (other_low, whole.at[48:72]),
        (other_high, whole.at[72:]),
        (early_at, early),
        (turned_at, turned),
        (same, whole.at[:48]),
    )
    pre[...] = jnp.zeros_like(pre)
    total[...] = jnp.zeros_like(total)
    part[:, 384:] = jnp.zeros((16, 16, 128), BF)
    for copy in copies[:3]:
        copy.wait()

    def slots(visit, step):
        def some(g, carry):
            for q in range(step):
                for j in range(4):
                    visit(g * step + q, j)
            return carry

        lax.fori_loop(0, 32 // step, some, 0)

    def block(d, j):
        lines = weights[d, j * 32 : (j + 1) * 32]
        return jnp.concatenate([lines[:, :BLK], lines[:, BLK:]], axis=0)

    forward_all(entries[0], 1, entries, weights, whole, pre)
    for copy in copies[3:]:
        copy.wait()
    unit = picker(False)

    def some_columns(g, carry):
        at = pl.multiple_of(g * 128, 128)
        v = (pre[pl.ds(g * 2, 2)] + early[pl.ds(g * 2, 2)]).reshape(128, 128)
        tangent = jnp.tanh(root_two_pi * (v + cubic_term * v * v * v))
        value = 0.5 * v * (1.0 + tangent)
        slope = 0.5 * (1.0 + tangent) + 0.5 * v * (1.0 - tangent * tangent) * root_two_pi * (
            1.0 + 3.0 * cubic_term * v * v
        )
        upstream = turned[pl.ds(g * 2, 2)].reshape(128, 128).astype(F32)
        grad[pl.ds(g * 2, 2)] = (upstream * slope).astype(BF).reshape(2, BLK, 128)
        hidden[:, pl.ds(at, 128)] = dot(unit, value.astype(BF), NT).astype(BF)
        return carry

    lax.fori_loop(0, 24, some_columns, 0, unroll=12)
    sent = [pltpu.make_async_copy(hidden, hidden_at, out_sems.at[16])]
    sent[-1].start()

    def weight(d, j):
        product = dot(whole[ids[d, j]], grad[ids[d, 4 + j]], NT).astype(BF)
        terms[d, j * 32 : (j + 1) * 32] = jnp.concatenate([product[:32], product[32:]], axis=1)

    slots(weight, 32)
    sent.append(pltpu.make_async_copy(terms, terms_at, out_sems.at[17]))
    sent[-1].start()

    def backward(d, j):
        total[ids[d, 8 + j]] += dot(block(d, j), grad[ids[d, 4 + j]])

    slots(backward, 32)
    for o in range(16):
        part[o, :384] = total[6 * o : 6 * o + 6].reshape(384, 128).astype(BF)
        here, size = (part.at[o], 400) if o < 15 else (part.at[o, :384], 384)
        sent.append(pltpu.make_async_copy(here, part_at.at[400 * o : 400 * o + size], out_sems.at[o]))
        sent[-1].start()
    for copy in sent:
        copy.wait()


def end_kernel(first, count_at, terms, own, weights, inputs, count, total, sems):
    [copy] = fetch(sems, (count_at, count))
    def some(d, kept):
        return kept + terms[d].astype(F32)

    kept = lax.fori_loop(1, terms.shape[0], some, terms[0].astype(F32))
    copy.wait()
    slot = first[0] + lax.broadcasted_iota(jnp.int32, (128, 128), 0) // 32
    total[...] = jnp.where(slot < count[0], kept, 0.0)
    for i in range(32):
        weights[0, :, i * 128 : (i + 1) * 128] = total[pl.ds(i, 4, stride=32), :].astype(BF)
    parted = picker(True)
    for k in range(3):
        at = k * 128
        inputs[:, at : at + 128] = dot(own[at : at + 128], parted, TN).astype(BF)


def shape(*dims):
    return jax.ShapeDtypeStruct(dims, BF)


def call(kernel, outs, n_scalar, n_array, scratch, flops, limit, place, leave):
    return pl.pallas_call(
        kernel,
        out_shape=outs,
        in_specs=[SM] * n_scalar + list(place if isinstance(place, tuple) else [place] * n_array),
        out_specs=leave,
        scratch_shapes=scratch,
        compiler_params=pltpu.CompilerParams(vmem_limit_bytes=limit * MIB),
        cost_estimate=pl.CostEstimate(flops=flops, bytes_accessed=2 * MIB, transcendentals=0),
    )


def on_device(tokens, weight_blocks, block_rows, block_columns, panel_counts, hidden_grad):
    n_row, n_col = lax.axis_size("row"), lax.axis_size(COL)
    me_row, me_col, me_side = lax.axis_index("row"), lax.axis_index(COL), lax.axis_index("side")
    first = (me_row * 4).reshape(1)

    def shift(a, by):
        return lax.ppermute(a, COL, [(i, (i + by) % n_col) for i in range(n_col)])

    parcels, turned = call(
        prep_kernel,
        (shape(n_row, 144, 128), shape(384, 128)),
        1,
        5,
        [
            pltpu.SMEM((1, 4), jnp.int32),
            pltpu.SMEM((1, 4), jnp.int32),
            pltpu.SMEM((1,), jnp.int32),
            pltpu.VMEM((1, 4, 4096), BF),
            pltpu.VMEM((128, 384), BF),
            pltpu.VMEM((128, 128), F32),
            pltpu.SemaphoreType.DMA((5,)),
        ],
        10_000_000,
        60,
        ANY,
        (VM, VM),
    )(first, block_rows, block_columns, panel_counts, weight_blocks, tokens)
    parcels = lax.all_to_all(parcels, "row", 0, 0, tiled=True)
    ids = parcels[:, 128, :8].astype(jnp.int32)
    owner = ids[:, :4] // 6
    rows = jnp.where(owner % 2 == me_side, 0, 48) + owner // 2 * 6 + ids[:, :4] % 6
    ids = jnp.concatenate([rows, ids[:, 4:], ids[:, :4]], axis=1)

    same = lax.all_gather(turned, "half", axis=0, tiled=True)
    middle = same.shape[0] // 2
    other_low, other_high = shift(same[:middle], 1), shift(same[middle:], -1)

    same, other_low, other_high = (a.reshape(-1, BLK, 128) for a in (same, other_low, other_high))
    early, turned, entries = call(
        early_kernel,
        (
            jax.ShapeDtypeStruct((48, BLK, 128), F32),
            shape(48, BLK, 128),
            jax.ShapeDtypeStruct((160,), jnp.int32),
        ),
        1,
        3,
        [
            pltpu.VMEM((n_row, 144, 128), BF),
            pltpu.VMEM((48, BLK, 128), BF),
            pltpu.VMEM((128, 3072), BF),
            pltpu.VMEM((49, BLK, 128), F32),
            pltpu.VMEM((48, BLK, 128), BF),
            pltpu.SMEM((160,), jnp.int32),
            pltpu.SemaphoreType.DMA((3,)),
            pltpu.SemaphoreType.DMA((2,)),
        ],
        500_000_000,
        8,
        ANY,
        (ANY, ANY, SM),
    )(ids, parcels, same, hidden_grad)

    hidden, part, terms = call(
        main_kernel,
        (shape(128, 3072), shape(6384, 128), shape(n_row, 128, 128)),
        2,
        6,
        [
            pltpu.VMEM((n_row, 144, 128), BF),
            pltpu.VMEM((96, BLK, 128), BF),
            pltpu.VMEM((48, BLK, 128), F32),
            pltpu.VMEM((48, BLK, 128), BF),
            pltpu.VMEM((128, 3072), BF),
            pltpu.VMEM((16, 400, 128), BF),
            pltpu.VMEM((n_row, 128, 128), BF),
            pltpu.VMEM((49, BLK, 128), F32),
            pltpu.VMEM((48, BLK, 128), BF),
            pltpu.VMEM((96, BLK, 128), F32),
            pltpu.SemaphoreType.DMA((6,)),
            pltpu.SemaphoreType.DMA((18,)),
        ],
        1_000_000_000,
        48,
        ANY,
        (ANY, ANY, ANY),
    )(ids, entries, parcels, same, other_low, other_high, early, turned)

    terms = lax.all_to_all(terms, "row", 0, 0, tiled=True)
    own = lax.optimization_barrier(lax.psum_scatter(part, COL, scatter_dimension=0, tiled=True))
    own = lax.dynamic_slice_in_dim(own, me_col, 384, 0)
    weight_grad, input_grad = call(
        end_kernel,
        (shape(1, 4, 4096), shape(128, 384)),
        1,
        3,
        [
            pltpu.SMEM((1,), jnp.int32),
            pltpu.VMEM((128, 128), F32),
            pltpu.SemaphoreType.DMA((1,)),
        ],
        10_000_000,
        4,
        (ANY, VM, VM),
        (VM, VM),
    )(first, panel_counts, terms, own)
    return hidden, input_grad, weight_grad


def solution(mesh):
    n_row, n_col = mesh.devices.shape
    fine = Mesh(mesh.devices.reshape(n_row, n_col // 2, 2), ("row", *COL))
    placed = (
        P("row", COL),
        P(COL, "row", None),
        P(COL, "row"),
        P(COL, "row"),
        P(COL),
        P("row", COL),
    )
    return jax.shard_map(
        on_device,
        mesh=fine,
        in_specs=placed,
        out_specs=(P("row", COL), P("row", COL), P(COL, "row", None)),
        check_vma=False,
    )
```

```python
import jax
import jax.numpy as jnp
from jax import lax
from jax.experimental import pallas as pl
from jax.experimental.pallas import tpu as pltpu
from jax.sharding import Mesh
from jax.sharding import PartitionSpec as P

root_two_pi = 0.7978845608028654
cubic_term = 0.044715
BF = jnp.bfloat16
F32 = jnp.float32
BLK = 64
NN = (((1,), (0,)), ((), ()))
NT = (((1,), (1,)), ((), ()))
TN = (((0,), (0,)), ((), ()))
COL = ("half", "side")
ALL = ("row", *COL)
SM = pl.BlockSpec(memory_space=pltpu.SMEM)
VM = pl.BlockSpec(memory_space=pltpu.VMEM)
ANY = pl.BlockSpec(memory_space=pl.ANY)
MIB = 1 << 20


def dot(a, b, dims=NN):
    return lax.dot_general(a, b, dims, preferred_element_type=F32)


def picker(parted):
    i = lax.broadcasted_iota(jnp.int32, (128, 128), 0)
    j = lax.broadcasted_iota(jnp.int32, (128, 128), 1)
    place = i // 64 * 64 + i % 32 * 2 + i % 64 // 32
    return ((place if parted else i) == j).astype(BF)


def fetch(sems, *pairs):
    copies = [pltpu.make_async_copy(a, b, sems.at[i]) for i, (a, b) in enumerate(pairs)]
    for copy in copies:
        copy.start()
    return copies


def prep_kernel(
    first, rows_at, columns_at, count_at, blocks_at, tokens_at, parcels, turned, rows, columns, count, blocks, tokens, spread, sems
):
    for copy in fetch(
        sems, (blocks_at, blocks), (tokens_at, tokens), (rows_at, rows), (columns_at, columns), (count_at, count)
    ):
        copy.wait()
    for i in range(32):
        spread[pl.ds(i, 4, stride=32), :] = blocks[0, :, i * 128 : (i + 1) * 128].astype(F32)
    slot = first[0] + lax.broadcasted_iota(jnp.int32, (128, 128), 0) // 32
    parcels[0, :128] = jnp.where(slot < count[0], spread[...], 0.0).astype(BF)
    lane = lax.broadcasted_iota(jnp.int32, (16, 128), 1)
    named = jnp.zeros((16, 128), jnp.int32)
    for j in range(4):
        named = jnp.where(lane == j, rows[0, j], named)
        named = jnp.where(lane == 4 + j, columns[0, j], named)
    parcels[0, 128:] = named.astype(F32).astype(BF)

    def again(d, carry):
        parcels[d] = parcels[0]
        return carry

    lax.fori_loop(1, parcels.shape[0], again, 0)
    parted = picker(True)
    for k in range(3):
        at = k * 128
        turned[at : at + 128] = dot(parted, tokens[:, at : at + 128], NT).astype(BF)


def forward(entry, weights, whole, pre):
    slot = jnp.bitwise_and(entry, 127)
    column = jnp.bitwise_and(jnp.right_shift(entry, 7), 63)
    row = jnp.right_shift(entry, 13)
    start = pl.multiple_of(jnp.bitwise_and(slot, 3) * 32, 32)
    lines = weights[jnp.right_shift(slot, 2), pl.ds(start, 32)]
    block = jnp.concatenate([lines[:, :BLK], lines[:, BLK:]], axis=0)
    pre[column] += dot(block, whole[row], TN)


def forward_all(count, at, entries, weights, whole, pre):
    def some(g, carry):
        for i in range(16):
            forward(entries[at + g * 16 + i], weights, whole, pre)
        return carry

    lax.fori_loop(0, jnp.right_shift(count + 15, 4), some, 0)


def early_kernel(
    ids,
    weights_at,
    same,
    upstream_at,
    early_at,
    turned_at,
    later,
    weights,
    whole,
    upstream,
    pre,
    turned,
    now,
    sems,
    out_sems,
):
    copies = fetch(sems, (upstream_at, upstream), (weights_at, weights), (same, whole))
    pre[...] = jnp.zeros_like(pre)

    def sort(d, counts):
        n, m = counts
        for j in range(4):
            row = ids[d, j]
            entry = (row * 64 + ids[d, 4 + j]) * 128 + d * 4 + j
            far = (row >= 48).astype(jnp.int32)
            now[n] = entry
            later[1 + m] = entry
            n, m = n + 1 - far, m + far
        return n, m

    n, m = lax.fori_loop(0, 32, sort, (jnp.int32(0), jnp.int32(0)))
    for i in range(16):
        now[n + i] = 48 * 128
        later[1 + m + i] = (48 * 64 + 48) * 128
    later[0] = m
    unit = picker(False)
    copies[0].wait()

    def some_columns(g, carry):
        at = pl.multiple_of(g * 128, 128)
        turned[pl.ds(g * 2, 2)] = dot(unit, upstream[:, pl.ds(at, 128)], NT).astype(BF).reshape(2, BLK, 128)
        return carry

    lax.fori_loop(0, 24, some_columns, 0, unroll=4)
    sent = fetch(out_sems.at[:1], (turned, turned_at))
    for copy in copies[1:]:
        copy.wait()
    forward_all(n, 0, now, weights, whole, pre)
    sent += fetch(out_sems.at[1:], (pre.at[:48], early_at))
    for copy in sent:
        copy.wait()


def main_kernel(
    ids,
    entries,
    weights_at,
    same,
    other_low,
    other_high,
    early_at,
    turned_at,
    hidden_at,
    part_at,
    terms_at,
    weights,
    whole,
    early,
    turned,
    hidden,
    part,
    terms,
    pre,
    grad,
    total,
    sems,
    out_sems,
):
    copies = fetch(
        sems,
        (weights_at, weights),
        (other_low, whole.at[48:72]),
        (other_high, whole.at[72:]),
        (early_at, early),
        (turned_at, turned),
        (same, whole.at[:48]),
    )
    pre[...] = jnp.zeros_like(pre)
    total[...] = jnp.zeros_like(total)
    part[:, 384:] = jnp.zeros((16, 16, 128), BF)
    for copy in copies[:3]:
        copy.wait()

    def slots(visit, step):
        def some(g, carry):
            for q in range(step):
                for j in range(4):
                    visit(g * step + q, j)
            return carry

        lax.fori_loop(0, 32 // step, some, 0)

    def block(d, j):
        lines = weights[d, j * 32 : (j + 1) * 32]
        return jnp.concatenate([lines[:, :BLK], lines[:, BLK:]], axis=0)

    forward_all(entries[0], 1, entries, weights, whole, pre)
    for copy in copies[3:]:
        copy.wait()
    unit = picker(False)

    def some_columns(g, carry):
        at = pl.multiple_of(g * 128, 128)
        v = (pre[pl.ds(g * 2, 2)] + early[pl.ds(g * 2, 2)]).reshape(128, 128)
        tangent = jnp.tanh(root_two_pi * (v + cubic_term * v * v * v))
        value = 0.5 * v * (1.0 + tangent)
        slope = 0.5 * (1.0 + tangent) + 0.5 * v * (1.0 - tangent * tangent) * root_two_pi * (
            1.0 + 3.0 * cubic_term * v * v
        )
        upstream = turned[pl.ds(g * 2, 2)].reshape(128, 128).astype(F32)
        grad[pl.ds(g * 2, 2)] = (upstream * slope).astype(BF).reshape(2, BLK, 128)
        hidden[:, pl.ds(at, 128)] = dot(unit, value.astype(BF), NT).astype(BF)
        return carry

    lax.fori_loop(0, 24, some_columns, 0, unroll=4)
    sent = [pltpu.make_async_copy(hidden, hidden_at, out_sems.at[16])]
    sent[-1].start()

    def weight(d, j):
        product = dot(whole[ids[d, j]], grad[ids[d, 4 + j]], NT).astype(BF)
        terms[d, j * 32 : (j + 1) * 32] = jnp.concatenate([product[:32], product[32:]], axis=1)

    slots(weight, 16)
    sent.append(pltpu.make_async_copy(terms, terms_at, out_sems.at[17]))
    sent[-1].start()

    def backward(d, j):
        total[ids[d, 8 + j]] += dot(block(d, j), grad[ids[d, 4 + j]])

    slots(backward, 16)
    for o in range(16):
        part[o, :384] = total[6 * o : 6 * o + 6].reshape(384, 128).astype(BF)
        here, size = (part.at[o], 400) if o < 15 else (part.at[o, :384], 384)
        sent.append(pltpu.make_async_copy(here, part_at.at[400 * o : 400 * o + size], out_sems.at[o]))
        sent[-1].start()
    for copy in sent:
        copy.wait()


def end_kernel(count, first, terms, own, weights, inputs, total):
    def some(d, kept):
        return kept + terms[d].astype(F32)

    kept = lax.fori_loop(1, terms.shape[0], some, terms[0].astype(F32))
    slot = first[0] + lax.broadcasted_iota(jnp.int32, (128, 128), 0) // 32
    total[...] = jnp.where(slot < count[0], kept, 0.0)
    for i in range(32):
        weights[0, :, i * 128 : (i + 1) * 128] = total[pl.ds(i, 4, stride=32), :].astype(BF)
    parted = picker(True)
    for k in range(3):
        at = k * 128
        inputs[:, at : at + 128] = dot(own[at : at + 128], parted, TN).astype(BF)


def shape(*dims):
    return jax.ShapeDtypeStruct(dims, BF)


def call(kernel, outs, n_scalar, n_array, scratch, flops, limit, place, leave):
    return pl.pallas_call(
        kernel,
        out_shape=outs,
        in_specs=[SM] * n_scalar + [place] * n_array,
        out_specs=leave,
        scratch_shapes=scratch,
        compiler_params=pltpu.CompilerParams(vmem_limit_bytes=limit * MIB),
        cost_estimate=pl.CostEstimate(flops=flops, bytes_accessed=2 * MIB, transcendentals=0),
    )


def on_device(tokens, weight_blocks, block_rows, block_columns, panel_counts, hidden_grad):
    n_row, n_col = lax.axis_size("row"), lax.axis_size(COL)
    me_row, me_col, me_side = lax.axis_index("row"), lax.axis_index(COL), lax.axis_index("side")
    first = (me_row * 4).reshape(1)

    def shift(a, by):
        return lax.ppermute(a, COL, [(i, (i + by) % n_col) for i in range(n_col)])

    def turn(group, row):
        return group[::-1] if row % 2 else group

    def mirrored(place, size):
        return jnp.where(me_row % 2 == 1, size - 1 - place, place)

    parcels, turned = call(
        prep_kernel,
        (shape(n_row, 144, 128), shape(384, 128)),
        1,
        5,
        [
            pltpu.SMEM((1, 4), jnp.int32),
            pltpu.SMEM((1, 4), jnp.int32),
            pltpu.SMEM((1,), jnp.int32),
            pltpu.VMEM((1, 4, 4096), BF),
            pltpu.VMEM((128, 384), BF),
            pltpu.VMEM((128, 128), F32),
            pltpu.SemaphoreType.DMA((5,)),
        ],
        10_000_000,
        60,
        ANY,
        (VM, VM),
    )(first, block_rows, block_columns, panel_counts, weight_blocks, tokens)
    parcels = lax.all_to_all(parcels, "row", 0, 0, tiled=True)
    ids = parcels[:, 128, :8].astype(jnp.int32)
    owner = ids[:, :4] // 6
    within = ids[:, :4] % 6
    near = mirrored(owner // 2, n_col // 2)
    rows = jnp.where(owner % 2 == me_side, 0, 48) + near * 6 + within
    sums = mirrored(owner, n_col) * 6 + within
    ids = jnp.concatenate([rows, ids[:, 4:], sums], axis=1)

    sides = [[r * n_col + h * 2 + s for h in range(n_col // 2)] for r in range(n_row) for s in range(2)]
    same = lax.all_gather(
        turned, ALL, axis=0, tiled=True, axis_index_groups=[turn(g, i // 2) for i, g in enumerate(sides)]
    )
    middle = same.shape[0] // 2
    other_low, other_high = shift(same[:middle], 1), shift(same[middle:], -1)

    same, other_low, other_high = (a.reshape(-1, BLK, 128) for a in (same, other_low, other_high))
    early, turned, entries = call(
        early_kernel,
        (
            jax.ShapeDtypeStruct((48, BLK, 128), F32),
            shape(48, BLK, 128),
            jax.ShapeDtypeStruct((160,), jnp.int32),
        ),
        1,
        3,
        [
            pltpu.VMEM((n_row, 144, 128), BF),
            pltpu.VMEM((48, BLK, 128), BF),
            pltpu.VMEM((128, 3072), BF),
            pltpu.VMEM((49, BLK, 128), F32),
            pltpu.VMEM((48, BLK, 128), BF),
            pltpu.SMEM((160,), jnp.int32),
            pltpu.SemaphoreType.DMA((3,)),
            pltpu.SemaphoreType.DMA((2,)),
        ],
        500_000_000,
        8,
        ANY,
        (ANY, ANY, SM),
    )(ids, parcels, same, hidden_grad)

    hidden, part, terms = call(
        main_kernel,
        (shape(128, 3072), shape(6384, 128), shape(n_row, 128, 128)),
        2,
        6,
        [
            pltpu.VMEM((n_row, 144, 128), BF),
            pltpu.VMEM((96, BLK, 128), BF),
            pltpu.VMEM((48, BLK, 128), F32),
            pltpu.VMEM((48, BLK, 128), BF),
            pltpu.VMEM((128, 3072), BF),
            pltpu.VMEM((16, 400, 128), BF),
            pltpu.VMEM((n_row, 128, 128), BF),
            pltpu.VMEM((49, BLK, 128), F32),
            pltpu.VMEM((48, BLK, 128), BF),
            pltpu.VMEM((96, BLK, 128), F32),
            pltpu.SemaphoreType.DMA((6,)),
            pltpu.SemaphoreType.DMA((18,)),
        ],
        1_000_000_000,
        48,
        ANY,
        (ANY, ANY, ANY),
    )(ids, entries, parcels, same, other_low, other_high, early, turned)

    terms = lax.all_to_all(terms, "row", 0, 0, tiled=True)
    lines = [turn(list(range(r * n_col, (r + 1) * n_col)), r) for r in range(n_row)]
    own = lax.optimization_barrier(
        lax.psum_scatter(part, ALL, scatter_dimension=0, tiled=True, axis_index_groups=lines)
    )
    own = lax.dynamic_slice_in_dim(own, mirrored(me_col, n_col), 384, 0)
    weight_grad, input_grad = call(
        end_kernel,
        (shape(1, 4, 4096), shape(128, 384)),
        2,
        2,
        [pltpu.VMEM((128, 128), F32)],
        10_000_000,
        4,
        VM,
        (VM, VM),
    )(panel_counts, first, terms, own)
    return hidden, input_grad, weight_grad


def solution(mesh):
    n_row, n_col = mesh.devices.shape
    fine = Mesh(mesh.devices.reshape(n_row, n_col // 2, 2), ("row", *COL))
    placed = (
        P("row", COL),
        P(COL, "row", None),
        P(COL, "row"),
        P(COL, "row"),
        P(COL),
        P("row", COL),
    )
    return jax.shard_map(
        on_device,
        mesh=fine,
        in_specs=placed,
        out_specs=(P("row", COL), P("row", COL), P(COL, "row", None)),
        check_vma=False,
    )
```

```python
import jax
import jax.numpy as jnp
from jax import lax
from jax.experimental import pallas as pl
from jax.experimental.pallas import tpu as pltpu
from jax.sharding import Mesh
from jax.sharding import PartitionSpec as P

root_two_pi = 0.7978845608028654
cubic_term = 0.044715
BF = jnp.bfloat16
F32 = jnp.float32
BLK = 64
NN = (((1,), (0,)), ((), ()))
NT = (((1,), (1,)), ((), ()))
TN = (((0,), (0,)), ((), ()))
COL = ("half", "side")
SM = pl.BlockSpec(memory_space=pltpu.SMEM)
VM = pl.BlockSpec(memory_space=pltpu.VMEM)
ANY = pl.BlockSpec(memory_space=pl.ANY)
MIB = 1 << 20


def dot(a, b, dims=NN):
    return lax.dot_general(a, b, dims, preferred_element_type=F32)


def picker(parted):
    i = lax.broadcasted_iota(jnp.int32, (128, 128), 0)
    j = lax.broadcasted_iota(jnp.int32, (128, 128), 1)
    place = i // 64 * 64 + i % 32 * 2 + i % 64 // 32
    return ((place if parted else i) == j).astype(BF)


def fetch(sems, *pairs):
    copies = [pltpu.make_async_copy(a, b, sems.at[i]) for i, (a, b) in enumerate(pairs)]
    for copy in copies:
        copy.start()
    return copies


def prep_kernel(
    first, rows_at, columns_at, count_at, blocks_at, tokens_at, parcels, turned, rows, columns, count, blocks, tokens, spread, sems
):
    for copy in fetch(
        sems, (blocks_at, blocks), (tokens_at, tokens), (rows_at, rows), (columns_at, columns), (count_at, count)
    ):
        copy.wait()
    for i in range(32):
        spread[pl.ds(i, 4, stride=32), :] = blocks[0, :, i * 128 : (i + 1) * 128].astype(F32)
    slot = first[0] + lax.broadcasted_iota(jnp.int32, (128, 128), 0) // 32
    parcels[0, :128] = jnp.where(slot < count[0], spread[...], 0.0).astype(BF)
    lane = lax.broadcasted_iota(jnp.int32, (16, 128), 1)
    named = jnp.zeros((16, 128), jnp.int32)
    for j in range(4):
        named = jnp.where(lane == j, rows[0, j], named)
        named = jnp.where(lane == 4 + j, columns[0, j], named)
    parcels[0, 128:] = named.astype(F32).astype(BF)

    def again(d, carry):
        parcels[d] = parcels[0]
        return carry

    lax.fori_loop(1, parcels.shape[0], again, 0)
    parted = picker(True)
    for k in range(3):
        at = k * 128
        turned[at : at + 128] = dot(parted, tokens[:, at : at + 128], NT).astype(BF)


def forward(entry, weights, whole, pre):
    slot = jnp.bitwise_and(entry, 127)
    column = jnp.bitwise_and(jnp.right_shift(entry, 7), 63)
    row = jnp.right_shift(entry, 13)
    start = pl.multiple_of(jnp.bitwise_and(slot, 3) * 32, 32)
    lines = weights[jnp.right_shift(slot, 2), pl.ds(start, 32)]
    block = jnp.concatenate([lines[:, :BLK], lines[:, BLK:]], axis=0)
    pre[column] += dot(block, whole[row], TN)


def forward_all(count, at, entries, weights, whole, pre):
    def some(g, carry):
        for i in range(16):
            forward(entries[at + g * 16 + i], weights, whole, pre)
        return carry

    lax.fori_loop(0, jnp.right_shift(count + 15, 4), some, 0)


def early_kernel(
    ids,
    weights_at,
    same,
    upstream_at,
    early_at,
    turned_at,
    later,
    weights,
    whole,
    upstream,
    pre,
    turned,
    now,
    sems,
    out_sems,
):
    copies = fetch(sems, (upstream_at, upstream), (weights_at, weights), (same, whole))
    pre[...] = jnp.zeros_like(pre)

    def sort(d, counts):
        n, m = counts
        for j in range(4):
            row = ids[d, j]
            entry = (row * 64 + ids[d, 4 + j]) * 128 + d * 4 + j
            far = (row >= 48).astype(jnp.int32)
            now[n] = entry
            later[1 + m] = entry
            n, m = n + 1 - far, m + far
        return n, m

    n, m = lax.fori_loop(0, 32, sort, (jnp.int32(0), jnp.int32(0)))
    for i in range(16):
        now[n + i] = 48 * 128
        later[1 + m + i] = (48 * 64 + 48) * 128
    later[0] = m
    unit = picker(False)
    copies[0].wait()

    def some_columns(g, carry):
        at = pl.multiple_of(g * 128, 128)
        turned[pl.ds(g * 2, 2)] = dot(unit, upstream[:, pl.ds(at, 128)], NT).astype(BF).reshape(2, BLK, 128)
        return carry

    lax.fori_loop(0, 24, some_columns, 0, unroll=4)
    sent = fetch(out_sems.at[:1], (turned, turned_at))
    for copy in copies[1:]:
        copy.wait()
    forward_all(n, 0, now, weights, whole, pre)
    sent += fetch(out_sems.at[1:], (pre.at[:48], early_at))
    for copy in sent:
        copy.wait()


def main_kernel(
    ids,
    entries,
    weights_at,
    same,
    other_low,
    other_high,
    early_at,
    turned_at,
    hidden_at,
    part_at,
    terms_at,
    weights,
    whole,
    early,
    turned,
    hidden,
    part,
    terms,
    pre,
    grad,
    total,
    sems,
    out_sems,
):
    copies = fetch(
        sems,
        (weights_at, weights),
        (other_low, whole.at[48:72]),
        (other_high, whole.at[72:]),
        (early_at, early),
        (turned_at, turned),
        (same, whole.at[:48]),
    )
    pre[...] = jnp.zeros_like(pre)
    total[...] = jnp.zeros_like(total)
    part[:, 384:] = jnp.zeros((16, 16, 128), BF)
    for copy in copies[:3]:
        copy.wait()

    def slots(visit, step):
        def some(g, carry):
            for q in range(step):
                for j in range(4):
                    visit(g * step + q, j)
            return carry

        lax.fori_loop(0, 32 // step, some, 0)

    def block(d, j):
        lines = weights[d, j * 32 : (j + 1) * 32]
        return jnp.concatenate([lines[:, :BLK], lines[:, BLK:]], axis=0)

    forward_all(entries[0], 1, entries, weights, whole, pre)
    for copy in copies[3:]:
        copy.wait()
    unit = picker(False)

    def some_columns(g, carry):
        at = pl.multiple_of(g * 128, 128)
        v = (pre[pl.ds(g * 2, 2)] + early[pl.ds(g * 2, 2)]).reshape(128, 128)
        tangent = jnp.tanh(root_two_pi * (v + cubic_term * v * v * v))
        value = 0.5 * v * (1.0 + tangent)
        slope = 0.5 * (1.0 + tangent) + 0.5 * v * (1.0 - tangent * tangent) * root_two_pi * (
            1.0 + 3.0 * cubic_term * v * v
        )
        upstream = turned[pl.ds(g * 2, 2)].reshape(128, 128).astype(F32)
        grad[pl.ds(g * 2, 2)] = (upstream * slope).astype(BF).reshape(2, BLK, 128)
        hidden[:, pl.ds(at, 128)] = dot(unit, value.astype(BF), NT).astype(BF)
        return carry

    lax.fori_loop(0, 24, some_columns, 0, unroll=8)
    sent = [pltpu.make_async_copy(hidden, hidden_at, out_sems.at[16])]
    sent[-1].start()

    def backward(d, j):
        total[ids[d, 8 + j]] += dot(block(d, j), grad[ids[d, 4 + j]])

    slots(backward, 16)
    for o in range(16):
        part[o, :384] = total[6 * o : 6 * o + 6].reshape(384, 128).astype(BF)
        here, size = (part.at[o], 400) if o < 15 else (part.at[o, :384], 384)
        sent.append(pltpu.make_async_copy(here, part_at.at[400 * o : 400 * o + size], out_sems.at[o]))
        sent[-1].start()

    def weight(d, j):
        product = dot(whole[ids[d, j]], grad[ids[d, 4 + j]], NT).astype(BF)
        terms[d, j * 32 : (j + 1) * 32] = jnp.concatenate([product[:32], product[32:]], axis=1)

    slots(weight, 16)
    sent.append(pltpu.make_async_copy(terms, terms_at, out_sems.at[17]))
    sent[-1].start()
    for copy in sent:
        copy.wait()


def end_kernel(count, first, terms, own, weights, inputs, total):
    def some(d, kept):
        return kept + terms[d].astype(F32)

    kept = lax.fori_loop(1, terms.shape[0], some, terms[0].astype(F32))
    slot = first[0] + lax.broadcasted_iota(jnp.int32, (128, 128), 0) // 32
    total[...] = jnp.where(slot < count[0], kept, 0.0)
    for i in range(32):
        weights[0, :, i * 128 : (i + 1) * 128] = total[pl.ds(i, 4, stride=32), :].astype(BF)
    parted = picker(True)
    for k in range(3):
        at = k * 128
        inputs[:, at : at + 128] = dot(own[at : at + 128], parted, TN).astype(BF)


def shape(*dims):
    return jax.ShapeDtypeStruct(dims, BF)


def call(kernel, outs, n_scalar, n_array, scratch, flops, limit, place, leave):
    return pl.pallas_call(
        kernel,
        out_shape=outs,
        in_specs=[SM] * n_scalar + [place] * n_array,
        out_specs=leave,
        scratch_shapes=scratch,
        compiler_params=pltpu.CompilerParams(vmem_limit_bytes=limit * MIB),
        cost_estimate=pl.CostEstimate(flops=flops, bytes_accessed=2 * MIB, transcendentals=0),
    )


def on_device(tokens, weight_blocks, block_rows, block_columns, panel_counts, hidden_grad):
    n_row, n_col = lax.axis_size("row"), lax.axis_size(COL)
    me_row, me_col, me_side = lax.axis_index("row"), lax.axis_index(COL), lax.axis_index("side")
    first = (me_row * 4).reshape(1)

    def shift(a, by):
        return lax.ppermute(a, COL, [(i, (i + by) % n_col) for i in range(n_col)])

    parcels, turned = call(
        prep_kernel,
        (shape(n_row, 144, 128), shape(384, 128)),
        1,
        5,
        [
            pltpu.SMEM((1, 4), jnp.int32),
            pltpu.SMEM((1, 4), jnp.int32),
            pltpu.SMEM((1,), jnp.int32),
            pltpu.VMEM((1, 4, 4096), BF),
            pltpu.VMEM((128, 384), BF),
            pltpu.VMEM((128, 128), F32),
            pltpu.SemaphoreType.DMA((5,)),
        ],
        10_000_000,
        60,
        ANY,
        (VM, VM),
    )(first, block_rows, block_columns, panel_counts, weight_blocks, tokens)
    parcels = lax.all_to_all(parcels, "row", 0, 0, tiled=True)
    ids = parcels[:, 128, :8].astype(jnp.int32)
    owner = ids[:, :4] // 6
    rows = jnp.where(owner % 2 == me_side, 0, 48) + owner // 2 * 6 + ids[:, :4] % 6
    ids = jnp.concatenate([rows, ids[:, 4:], ids[:, :4]], axis=1)

    same = lax.all_gather(turned, "half", axis=0, tiled=True)
    middle = same.shape[0] // 2
    other_low, other_high = shift(same[:middle], 1), shift(same[middle:], -1)

    same, other_low, other_high = (a.reshape(-1, BLK, 128) for a in (same, other_low, other_high))
    early, turned, entries = call(
        early_kernel,
        (
            jax.ShapeDtypeStruct((48, BLK, 128), F32),
            shape(48, BLK, 128),
            jax.ShapeDtypeStruct((160,), jnp.int32),
        ),
        1,
        3,
        [
            pltpu.VMEM((n_row, 144, 128), BF),
            pltpu.VMEM((48, BLK, 128), BF),
            pltpu.VMEM((128, 3072), BF),
            pltpu.VMEM((49, BLK, 128), F32),
            pltpu.VMEM((48, BLK, 128), BF),
            pltpu.SMEM((160,), jnp.int32),
            pltpu.SemaphoreType.DMA((3,)),
            pltpu.SemaphoreType.DMA((2,)),
        ],
        500_000_000,
        8,
        ANY,
        (ANY, ANY, SM),
    )(ids, parcels, same, hidden_grad)

    hidden, part, terms = call(
        main_kernel,
        (shape(128, 3072), shape(6384, 128), shape(n_row, 128, 128)),
        2,
        6,
        [
            pltpu.VMEM((n_row, 144, 128), BF),
            pltpu.VMEM((96, BLK, 128), BF),
            pltpu.VMEM((48, BLK, 128), F32),
            pltpu.VMEM((48, BLK, 128), BF),
            pltpu.VMEM((128, 3072), BF),
            pltpu.VMEM((16, 400, 128), BF),
            pltpu.VMEM((n_row, 128, 128), BF),
            pltpu.VMEM((49, BLK, 128), F32),
            pltpu.VMEM((48, BLK, 128), BF),
            pltpu.VMEM((96, BLK, 128), F32),
            pltpu.SemaphoreType.DMA((6,)),
            pltpu.SemaphoreType.DMA((18,)),
        ],
        1_000_000_000,
        48,
        ANY,
        (ANY, ANY, ANY),
    )(ids, entries, parcels, same, other_low, other_high, early, turned)

    terms = lax.all_to_all(terms, "row", 0, 0, tiled=True)
    own = lax.optimization_barrier(lax.psum_scatter(part, COL, scatter_dimension=0, tiled=True))
    own = lax.dynamic_slice_in_dim(own, me_col, 384, 0)
    weight_grad, input_grad = call(
        end_kernel,
        (shape(1, 4, 4096), shape(128, 384)),
        2,
        2,
        [pltpu.VMEM((128, 128), F32)],
        10_000_000,
        4,
        VM,
        (VM, VM),
    )(panel_counts, first, terms, own)
    return hidden, input_grad, weight_grad


def solution(mesh):
    n_row, n_col = mesh.devices.shape
    fine = Mesh(mesh.devices.reshape(n_row, n_col // 2, 2), ("row", *COL))
    placed = (
        P("row", COL),
        P(COL, "row", None),
        P(COL, "row"),
        P(COL, "row"),
        P(COL),
        P("row", COL),
    )
    return jax.shard_map(
        on_device,
        mesh=fine,
        in_specs=placed,
        out_specs=(P("row", COL), P("row", COL), P(COL, "row", None)),
        check_vma=False,
    )
```

```python
import jax
import jax.numpy as jnp
from jax import lax
from jax.experimental import pallas as pl
from jax.experimental.pallas import tpu as pltpu
from jax.sharding import Mesh
from jax.sharding import PartitionSpec as P

root_two_pi = 0.7978845608028654
cubic_term = 0.044715
BF = jnp.bfloat16
F32 = jnp.float32
BLK = 64
NN = (((1,), (0,)), ((), ()))
NT = (((1,), (1,)), ((), ()))
TN = (((0,), (0,)), ((), ()))
COL = ("half", "side")
SM = pl.BlockSpec(memory_space=pltpu.SMEM)
VM = pl.BlockSpec(memory_space=pltpu.VMEM)
ANY = pl.BlockSpec(memory_space=pl.ANY)
MIB = 1 << 20


def dot(a, b, dims=NN):
    return lax.dot_general(a, b, dims, preferred_element_type=F32)


def picker(parted):
    i = lax.broadcasted_iota(jnp.int32, (128, 128), 0)
    j = lax.broadcasted_iota(jnp.int32, (128, 128), 1)
    place = i // 64 * 64 + i % 32 * 2 + i % 64 // 32
    return ((place if parted else i) == j).astype(BF)


def fetch(sems, *pairs):
    copies = [pltpu.make_async_copy(a, b, sems.at[i]) for i, (a, b) in enumerate(pairs)]
    for copy in copies:
        copy.start()
    return copies


def prep_kernel(
    first, rows_at, columns_at, count_at, blocks_at, tokens_at, parcels, turned, rows, columns, count, blocks, tokens, spread, sems
):
    for copy in fetch(
        sems, (blocks_at, blocks), (tokens_at, tokens), (rows_at, rows), (columns_at, columns), (count_at, count)
    ):
        copy.wait()
    for i in range(32):
        spread[pl.ds(i, 4, stride=32), :] = blocks[0, :, i * 128 : (i + 1) * 128].astype(F32)
    slot = first[0] + lax.broadcasted_iota(jnp.int32, (128, 128), 0) // 32
    parcels[0, :128] = jnp.where(slot < count[0], spread[...], 0.0).astype(BF)
    lane = lax.broadcasted_iota(jnp.int32, (16, 128), 1)
    named = jnp.zeros((16, 128), jnp.int32)
    for j in range(4):
        named = jnp.where(lane == j, rows[0, j], named)
        named = jnp.where(lane == 4 + j, columns[0, j], named)
    parcels[0, 128:] = named.astype(F32).astype(BF)

    def again(d, carry):
        parcels[d] = parcels[0]
        return carry

    lax.fori_loop(1, parcels.shape[0], again, 0)
    parted = picker(True)
    for k in range(3):
        at = k * 128
        turned[at : at + 128] = dot(parted, tokens[:, at : at + 128], NT).astype(BF)


def forward(entry, weights, whole, pre):
    slot = jnp.bitwise_and(entry, 127)
    column = jnp.bitwise_and(jnp.right_shift(entry, 7), 63)
    row = jnp.right_shift(entry, 13)
    start = pl.multiple_of(jnp.bitwise_and(slot, 3) * 32, 32)
    lines = weights[jnp.right_shift(slot, 2), pl.ds(start, 32)]
    block = jnp.concatenate([lines[:, :BLK], lines[:, BLK:]], axis=0)
    pre[column] += dot(block, whole[row], TN)


def forward_all(count, at, entries, weights, whole, pre):
    def some(g, carry):
        for i in range(16):
            forward(entries[at + g * 16 + i], weights, whole, pre)
        return carry

    lax.fori_loop(0, jnp.right_shift(count + 15, 4), some, 0)


def early_kernel(
    ids,
    weights_at,
    same,
    upstream_at,
    early_at,
    turned_at,
    later,
    weights,
    whole,
    upstream,
    pre,
    turned,
    now,
    sems,
    out_sems,
):
    copies = fetch(sems, (upstream_at, upstream), (weights_at, weights), (same, whole))
    pre[...] = jnp.zeros_like(pre)

    def sort(d, counts):
        n, m = counts
        for j in range(4):
            row = ids[d, j]
            entry = (row * 64 + ids[d, 4 + j]) * 128 + d * 4 + j
            far = (row >= 48).astype(jnp.int32)
            now[n] = entry
            later[1 + m] = entry
            n, m = n + 1 - far, m + far
        return n, m

    n, m = lax.fori_loop(0, 32, sort, (jnp.int32(0), jnp.int32(0)))
    for i in range(16):
        now[n + i] = 48 * 128
        later[1 + m + i] = (48 * 64 + 48) * 128
    later[0] = m
    unit = picker(False)
    copies[0].wait()

    def some_columns(g, carry):
        at = pl.multiple_of(g * 128, 128)
        turned[pl.ds(g * 2, 2)] = dot(unit, upstream[:, pl.ds(at, 128)], NT).astype(BF).reshape(2, BLK, 128)
        return carry

    lax.fori_loop(0, 24, some_columns, 0, unroll=4)
    sent = fetch(out_sems.at[:1], (turned, turned_at))
    for copy in copies[1:]:
        copy.wait()
    forward_all(n, 0, now, weights, whole, pre)
    sent += fetch(out_sems.at[1:], (pre.at[:48], early_at))
    for copy in sent:
        copy.wait()


def main_kernel(
    ids,
    entries,
    weights_at,
    same,
    other_low,
    other_high,
    early_at,
    turned_at,
    hidden_at,
    part_at,
    terms_at,
    weights,
    whole,
    early,
    turned,
    hidden,
    part,
    terms,
    pre,
    grad,
    total,
    sems,
    out_sems,
):
    copies = fetch(
        sems,
        (weights_at, weights),
        (other_low, whole.at[48:72]),
        (other_high, whole.at[72:]),
        (early_at, early),
        (turned_at, turned),
        (same, whole.at[:48]),
    )
    pre[...] = jnp.zeros_like(pre)
    total[...] = jnp.zeros_like(total)
    part[:, 384:] = jnp.zeros((16, 16, 128), BF)
    for copy in copies[:3]:
        copy.wait()

    def slots(visit, step):
        def some(g, carry):
            for q in range(step):
                for j in range(4):
                    visit(g * step + q, j)
            return carry

        lax.fori_loop(0, 32 // step, some, 0)

    def block(d, j):
        lines = weights[d, j * 32 : (j + 1) * 32]
        return jnp.concatenate([lines[:, :BLK], lines[:, BLK:]], axis=0)

    forward_all(entries[0], 1, entries, weights, whole, pre)
    for copy in copies[3:]:
        copy.wait()
    unit = picker(False)

    def some_columns(g, carry):
        at = pl.multiple_of(g * 128, 128)
        v = (pre[pl.ds(g * 2, 2)] + early[pl.ds(g * 2, 2)]).reshape(128, 128)
        tangent = jnp.tanh(root_two_pi * (v + cubic_term * v * v * v))
        value = 0.5 * v * (1.0 + tangent)
        slope = 0.5 * (1.0 + tangent) + 0.5 * v * (1.0 - tangent * tangent) * root_two_pi * (
            1.0 + 3.0 * cubic_term * v * v
        )
        upstream = turned[pl.ds(g * 2, 2)].reshape(128, 128).astype(F32)
        grad[pl.ds(g * 2, 2)] = (upstream * slope).astype(BF).reshape(2, BLK, 128)
        hidden[:, pl.ds(at, 128)] = dot(unit, value.astype(BF), NT).astype(BF)
        return carry

    lax.fori_loop(0, 24, some_columns, 0, unroll=8)
    sent = [pltpu.make_async_copy(hidden, hidden_at, out_sems.at[16])]
    sent[-1].start()

    def backward(d, j):
        total[ids[d, 8 + j]] += dot(block(d, j), grad[ids[d, 4 + j]])

    slots(backward, 16)
    for o in range(16):
        part[o, :384] = total[6 * o : 6 * o + 6].reshape(384, 128).astype(BF)
        here, size = (part.at[o], 400) if o < 15 else (part.at[o, :384], 384)
        sent.append(pltpu.make_async_copy(here, part_at.at[400 * o : 400 * o + size], out_sems.at[o]))
        sent[-1].start()

    def weight(d, j):
        product = dot(whole[ids[d, j]], grad[ids[d, 4 + j]], NT).astype(BF)
        terms[d, j * 32 : (j + 1) * 32] = jnp.concatenate([product[:32], product[32:]], axis=1)

    slots(weight, 32)
    sent.append(pltpu.make_async_copy(terms, terms_at, out_sems.at[17]))
    sent[-1].start()
    for copy in sent:
        copy.wait()


def end_kernel(count, first, terms, own, weights, inputs, total):
    def some(d, kept):
        return kept + terms[d].astype(F32)

    kept = lax.fori_loop(1, terms.shape[0], some, terms[0].astype(F32), unroll=31)
    slot = first[0] + lax.broadcasted_iota(jnp.int32, (128, 128), 0) // 32
    total[...] = jnp.where(slot < count[0], kept, 0.0)
    for i in range(32):
        weights[0, :, i * 128 : (i + 1) * 128] = total[pl.ds(i, 4, stride=32), :].astype(BF)
    parted = picker(True)
    for k in range(3):
        at = k * 128
        inputs[:, at : at + 128] = dot(own[at : at + 128], parted, TN).astype(BF)


def shape(*dims):
    return jax.ShapeDtypeStruct(dims, BF)


def call(kernel, outs, n_scalar, n_array, scratch, flops, limit, place, leave):
    return pl.pallas_call(
        kernel,
        out_shape=outs,
        in_specs=[SM] * n_scalar + [place] * n_array,
        out_specs=leave,
        scratch_shapes=scratch,
        compiler_params=pltpu.CompilerParams(vmem_limit_bytes=limit * MIB),
        cost_estimate=pl.CostEstimate(flops=flops, bytes_accessed=2 * MIB, transcendentals=0),
    )


def on_device(tokens, weight_blocks, block_rows, block_columns, panel_counts, hidden_grad):
    n_row, n_col = lax.axis_size("row"), lax.axis_size(COL)
    me_row, me_col, me_side = lax.axis_index("row"), lax.axis_index(COL), lax.axis_index("side")
    first = (me_row * 4).reshape(1)

    def shift(a, by):
        return lax.ppermute(a, COL, [(i, (i + by) % n_col) for i in range(n_col)])

    parcels, turned = call(
        prep_kernel,
        (shape(n_row, 144, 128), shape(384, 128)),
        1,
        5,
        [
            pltpu.SMEM((1, 4), jnp.int32),
            pltpu.SMEM((1, 4), jnp.int32),
            pltpu.SMEM((1,), jnp.int32),
            pltpu.VMEM((1, 4, 4096), BF),
            pltpu.VMEM((128, 384), BF),
            pltpu.VMEM((128, 128), F32),
            pltpu.SemaphoreType.DMA((5,)),
        ],
        10_000_000,
        60,
        ANY,
        (VM, VM),
    )(first, block_rows, block_columns, panel_counts, weight_blocks, tokens)
    parcels = lax.all_to_all(parcels, "row", 0, 0, tiled=True)
    ids = parcels[:, 128, :8].astype(jnp.int32)
    owner = ids[:, :4] // 6
    rows = jnp.where(owner % 2 == me_side, 0, 48) + owner // 2 * 6 + ids[:, :4] % 6
    ids = jnp.concatenate([rows, ids[:, 4:], ids[:, :4]], axis=1)

    same = lax.all_gather(turned, "half", axis=0, tiled=True)
    middle = same.shape[0] // 2
    other_low, other_high = shift(same[:middle], 1), shift(same[middle:], -1)

    same, other_low, other_high = (a.reshape(-1, BLK, 128) for a in (same, other_low, other_high))
    early, turned, entries = call(
        early_kernel,
        (
            jax.ShapeDtypeStruct((48, BLK, 128), F32),
            shape(48, BLK, 128),
            jax.ShapeDtypeStruct((160,), jnp.int32),
        ),
        1,
        3,
        [
            pltpu.VMEM((n_row, 144, 128), BF),
            pltpu.VMEM((48, BLK, 128), BF),
            pltpu.VMEM((128, 3072), BF),
            pltpu.VMEM((49, BLK, 128), F32),
            pltpu.VMEM((48, BLK, 128), BF),
            pltpu.SMEM((160,), jnp.int32),
            pltpu.SemaphoreType.DMA((3,)),
            pltpu.SemaphoreType.DMA((2,)),
        ],
        500_000_000,
        8,
        ANY,
        (ANY, ANY, SM),
    )(ids, parcels, same, hidden_grad)

    hidden, part, terms = call(
        main_kernel,
        (shape(128, 3072), shape(6384, 128), shape(n_row, 128, 128)),
        2,
        6,
        [
            pltpu.VMEM((n_row, 144, 128), BF),
            pltpu.VMEM((96, BLK, 128), BF),
            pltpu.VMEM((48, BLK, 128), F32),
            pltpu.VMEM((48, BLK, 128), BF),
            pltpu.VMEM((128, 3072), BF),
            pltpu.VMEM((16, 400, 128), BF),
            pltpu.VMEM((n_row, 128, 128), BF),
            pltpu.VMEM((49, BLK, 128), F32),
            pltpu.VMEM((48, BLK, 128), BF),
            pltpu.VMEM((96, BLK, 128), F32),
            pltpu.SemaphoreType.DMA((6,)),
            pltpu.SemaphoreType.DMA((18,)),
        ],
        1_000_000_000,
        48,
        ANY,
        (ANY, ANY, ANY),
    )(ids, entries, parcels, same, other_low, other_high, early, turned)

    terms = lax.all_to_all(terms, "row", 0, 0, tiled=True)
    own = lax.optimization_barrier(lax.psum_scatter(part, COL, scatter_dimension=0, tiled=True))
    own = lax.dynamic_slice_in_dim(own, me_col, 384, 0)
    weight_grad, input_grad = call(
        end_kernel,
        (shape(1, 4, 4096), shape(128, 384)),
        2,
        2,
        [pltpu.VMEM((128, 128), F32)],
        10_000_000,
        4,
        VM,
        (VM, VM),
    )(panel_counts, first, terms, own)
    return hidden, input_grad, weight_grad


def solution(mesh):
    n_row, n_col = mesh.devices.shape
    fine = Mesh(mesh.devices.reshape(n_row, n_col // 2, 2), ("row", *COL))
    placed = (
        P("row", COL),
        P(COL, "row", None),
        P(COL, "row"),
        P(COL, "row"),
        P(COL),
        P("row", COL),
    )
    return jax.shard_map(
        on_device,
        mesh=fine,
        in_specs=placed,
        out_specs=(P("row", COL), P("row", COL), P(COL, "row", None)),
        check_vma=False,
    )
```
